32 devices in a mesh: groups: 2 (over y), users: 4 (over z), mp: 2 (over x), helpers: 2 (over core).
Axes of the slice: x: 2, y: 2, z: 4, core: 2. Of those that a mesh axis runs over, the one named last changes fastest.
Arguments:
- candidates: bfloat16 [32, 128, 1024], P(('groups', 'users', 'helpers')), parts along dimension 0, may hold values from -6 to 6
- block_user: int32 [32], P(('groups', 'users', 'helpers')), parts along dimension 0, may hold values from 0 to 31, as said below
- block_count: int32 [32], P(('groups', 'users', 'helpers')), parts along dimension 0, may hold values from 16 to 32, as said below
- own_map: int32 [64], P('groups'), parts along dimension 0, may hold values from 0 to 31, as said below
- history_key_cache: bfloat16 [64, 512, 1024], P(('groups', 'users'), None, 'mp'), parts along dimension 0, may hold values from -6 to 6
- cache_values: bfloat16 [64, 512, 1024], P(('groups', 'users'), None, 'mp'), parts along dimension 0, may hold values from -64 to 64
- w_query_unit: bfloat16 [2, 1024, 1024], P(None, None, 'mp'), may hold values from -0.1875 to 0.1875
- time_bias: float32 [8, 512], P('mp'), may hold values from -5 to 5
- output_weight: bfloat16 [1024, 1024], P('mp'), may hold values from -0.1875 to 0.1875
- w_score: float32 [1024], P('mp'), may hold values from -0.1875 to 0.1875
Outputs:
- scores: float32 [32, 128], P(('groups', 'users', 'helpers')), parts along dimension 0
The draws below stay inside these ranges and needn't reach their ends.
There are 2 independent parts, one for each index of `groups`. The reference program is written for one: setup_inputs(seed, part) draws one part's arguments, and reference() takes and returns one part's arrays. A program takes and returns all parts, laid end to end along the dimension named above; an argument that names none is the same for every part. Nothing has to cross between parts.
Inputs may be any that keep to these rules, and one draw needn't show every extreme that they name: own_map is a permutation of the users; user u's history is row own_map[u] of the caches. `block_user`: the 2 blocks of one device belong to users whose cache rows, divided by 8, are all different; in every draw one such quotient is that of a block on every device. `block_count`: on every device some block has exactly 32 live candidates.
All inputs are finite; a program needn't handle non-finite values.
Results may differ from the reference program's by a relative error of at most 0.003.
Values may be sent and summed in bfloat16 or wider, within the bound.
No kernel may reach another device: no remote copies, remote signals or barrier semaphores. Data moves between devices by JAX's collectives and lax.ppermute only.
A program may use at most 128 MiB of HBM per device.

```python
import math
import jax
import jax.numpy as jnp
from jax import lax

D = 1024
H = 8
L = 512
U_DEV = 8
BLOCK = 128
MOST = 32
OWNERS = 4
SOURCES = 8
B_DEV = 2
BLOCKS = 16
USERS = 32


def routing_plan(key):
    anchor = jax.random.fold_in(key, 7)
    owner_perm = jax.random.permutation(jax.random.fold_in(anchor, 1), USERS).astype(jnp.int32)
    hottest = jax.random.randint(jax.random.fold_in(anchor, 2), (), 0, OWNERS).astype(jnp.int32)
    source_keys = jax.random.split(jax.random.fold_in(anchor, 3), SOURCES)

    def one_source(source_key):
        leading_key = jax.random.fold_in(source_key, 1)
        second_key = jax.random.fold_in(source_key, 2)
        third_key = jax.random.fold_in(source_key, 3)
        others = jax.random.permutation(leading_key, OWNERS - 1).astype(jnp.int32)
        others = others + (others >= hottest).astype(jnp.int32)
        targets = jnp.concatenate([hottest[None], others])[:B_DEV]
        row_permuter = jax.random.permutation(second_key, B_DEV)
        targets = targets[row_permuter]
        local_slot = jax.random.randint(third_key, (B_DEV,), 0, U_DEV).astype(jnp.int32)
        return targets * U_DEV + local_slot
    row_ids = jax.vmap(one_source)(source_keys).reshape(-1)
    inverse = jnp.zeros((USERS,), jnp.int32).at[owner_perm].set(jnp.arange(USERS, dtype=jnp.int32))
    user_ids = inverse[row_ids]
    return (owner_perm, user_ids.astype(jnp.int32))


def draw_own_map(key, part):
    return routing_plan(key)[0]


def draw_block_user(key, part):
    return routing_plan(key)[1]


def draw_block_count(key, part):
    counted = jax.random.randint(jax.random.fold_in(key, 11), (SOURCES, B_DEV), MOST // 2, MOST + 1).astype(jnp.int32)
    fullest = jax.random.randint(jax.random.fold_in(key, 12), (SOURCES, 1), 0, B_DEV).astype(jnp.int32)
    column_ids = jnp.arange(B_DEV, dtype=jnp.int32)[None, :]
    counted = jnp.where(column_ids == fullest, MOST, counted)
    return counted.reshape(-1).astype(jnp.int32)


def draw_cache_values(key, part):
    leading_key = jax.random.fold_in(key, 21)
    second_key = jax.random.fold_in(key, 22)
    scales = jnp.exp(jax.random.uniform(leading_key, (USERS, 1, D), jnp.float32, 0.0, math.log(10.0)))
    noise = jnp.clip(jax.random.normal(second_key, (USERS, L, D), jnp.float32), -4.0, 4.0)
    drawn = noise * scales
    return drawn.astype(jnp.bfloat16)


def block_scale(stream_key, dims, shards, smallest, top_value):
    def one(position, parts):
        draws = jax.random.uniform(jax.random.fold_in(jax.random.fold_in(stream_key, 6), position), (parts,), jnp.float32, smallest / len(shards), top_value / len(shards))
        return jnp.repeat(jnp.exp(draws), dims[position] // parts).reshape((-1,) + (1,) * (len(dims) - position - 1))

    level = one(*shards[0])
    for cut in shards[1:]:
        level = level * one(*cut)
    return level


def bell_draw(stream_key, shape, scale, limit, cuts=(), held_as=jnp.bfloat16):
    array = jax.random.normal(stream_key, shape, jnp.float32) * scale
    if len(cuts) > 0:
        array = block_scale(stream_key, shape, cuts, -0.22, 0.18) * array
    return jnp.clip(array, min=-limit, max=limit).astype(held_as)


def setup_inputs(seed: int = 0, part: int = 0) -> dict:
    splits = jax.random.split(jax.random.key(seed), 11)
    own_keys = jax.random.split(jax.random.fold_in(splits[10], part), 11)
    return {
        "candidates": bell_draw(own_keys[0], (BLOCKS, BLOCK, D), 1.0, 6.0, ((0, 8),)),
        "block_user": draw_block_user(jax.random.fold_in(jax.random.fold_in(splits[10], part), 71), part),
        "block_count": draw_block_count(jax.random.fold_in(jax.random.fold_in(splits[10], part), 71), part),
        "own_map": draw_own_map(jax.random.fold_in(jax.random.fold_in(splits[10], part), 71), part),
        "history_key_cache": bell_draw(own_keys[4], (USERS, L, D), 1.0, 6.0, ((0, 4), (2, 2))),
        "cache_values": draw_cache_values(jax.random.fold_in(jax.random.fold_in(splits[10], part), 71), part),
        "w_query_unit": bell_draw(splits[6], (2, D, D), D ** -0.5, 0.1875, ((2, 2),)),
        "time_bias": bell_draw(splits[7], (H, L), 1.0, 5.0, ((0, 2),), jnp.float32),
        "output_weight": bell_draw(splits[8], (D, D), D ** -0.5, 0.1875, ((0, 2),)),
        "w_score": bell_draw(splits[9], (D,), D ** -0.5, 0.1875, ((0, 2),), jnp.float32),
    }


EPSILON = 1e-05

def reference(candidates, block_user, block_count, own_map, history_key_cache, cache_values, w_query_unit, time_bias, output_weight, w_score):
    heads = time_bias.shape[0]
    model_width = candidates.shape[2]
    head_size = model_width // heads
    storage = own_map[block_user].astype(jnp.int32)

    def one_block(block_item):
        block_rows_in, live_count, row_index = block_item
        block_rows_in = block_rows_in[:MOST]
        query_bf = jax.nn.silu(jnp.dot(block_rows_in, w_query_unit[0], preferred_element_type=jnp.float32)).astype(jnp.bfloat16)
        unit_gate = jax.nn.silu(jnp.dot(block_rows_in, w_query_unit[1], preferred_element_type=jnp.float32))
        key_rows = lax.dynamic_index_in_dim(history_key_cache, row_index, 0, keepdims=False)
        value_rows = lax.dynamic_index_in_dim(cache_values, row_index, 0, keepdims=False)
        query_heads = lax.optimization_barrier(query_bf).astype(jnp.float32).reshape(MOST, heads, head_size)
        key_heads = key_rows.astype(jnp.float32).reshape(-1, heads, head_size)
        value_heads = value_rows.astype(jnp.float32).reshape(-1, heads, head_size)
        logits = jnp.einsum('nhd,lhd->hnl', query_heads, key_heads) * head_size ** (-0.5) + time_bias[:, None, :]
        weight_bf = jax.nn.silu(logits).astype(jnp.bfloat16)
        weights = lax.optimization_barrier(weight_bf).astype(jnp.float32)
        mixture = jnp.einsum('hnl,lhd->nhd', weights, value_heads).reshape(MOST, model_width)
        row_mean = lax.optimization_barrier(jnp.mean(mixture, axis=1, keepdims=True))
        spread = lax.optimization_barrier(jnp.mean(mixture * mixture, axis=1, keepdims=True)) - row_mean * row_mean
        normed = (mixture - row_mean) * lax.rsqrt(spread + EPSILON)
        gate_applied_rows = (normed * unit_gate).astype(jnp.bfloat16)
        out_rows = jnp.dot(gate_applied_rows, output_weight, preferred_element_type=jnp.float32)
        block_scores = lax.optimization_barrier(jnp.sum(jax.nn.silu(block_rows_in.astype(jnp.float32) + out_rows) * w_score, axis=1))
        live_mask = jnp.arange(MOST, dtype=jnp.int32) < live_count
        block_scores = jnp.where(live_mask, block_scores, jnp.zeros_like(block_scores))
        return jnp.concatenate([block_scores, jnp.zeros((BLOCK - MOST,), block_scores.dtype)])
    return lax.map(one_block, (candidates, block_count, storage), batch_size=8)
```

```python
import functools

import jax
import jax.numpy as jnp
from jax import lax
from jax.experimental import pallas as pl
from jax.experimental.pallas import tpu as pltpu
from jax.sharding import PartitionSpec as P

EPSILON = 1e-05
MOST = 32
LANES = 128
F32 = jnp.float32
BF16 = jnp.bfloat16
VMEM = pl.BlockSpec(memory_space=pltpu.VMEM)
SMEM = pl.BlockSpec(memory_space=pltpu.SMEM)
ANY = pl.BlockSpec(memory_space=pl.ANY)


def silu(v):
    return v / (1.0 + jnp.exp(-v))


def split3(v):
    high = v.astype(BF16).astype(F32)
    rest = v - high
    middle = rest.astype(BF16).astype(F32)
    return high, middle, rest - middle


def in_lanes(columns, rows):
    lane = lax.broadcasted_iota(jnp.int32, (rows, LANES), 1)
    tail = jnp.zeros((rows, LANES), F32)
    for position, column in enumerate(columns):
        tail = jnp.where(lane == position, column, tail)
    return tail


def joined(tail, first):
    return tail[:, first : first + 1] + tail[:, first + 1 : first + 2] + tail[:, first + 2 : first + 3]


def placed(block_user, own_map, block, users_here):
    storage = own_map[block_user[block]]
    return storage // users_here, storage % users_here


def query_kernel(owners, users_here, block_user, own_map, me, candidates, weights, *rest):
    slots = rest[:owners]
    x, w, x_sems, w_sem = rest[owners:]
    blocks = candidates.shape[0]
    width = w.shape[1]
    w_copy = pltpu.make_async_copy(weights.at[0], w, w_sem)
    w_copy.start()
    x_copies = [
        pltpu.make_async_copy(
            candidates.at[b, pl.ds(0, MOST)], x.at[pl.ds(b * MOST, MOST)], x_sems.at[b]
        )
        for b in range(blocks)
    ]
    for copy in x_copies:
        copy.start()
    for copy in x_copies:
        copy.wait()
    w_copy.wait()
    query = silu(jnp.dot(x[...], w[...], preferred_element_type=F32)).astype(BF16)
    homes = [placed(block_user, own_map, b, users_here) for b in range(blocks)]
    for s in range(owners):
        slot = jnp.zeros((MOST, width), BF16)
        tag = jnp.zeros((MOST, LANES), F32)
        for b, (owner, row) in enumerate(homes):
            here = (owner ^ me[0]) == s
            slot = jnp.where(here, query[b * MOST : (b + 1) * MOST], slot)
            tag = jnp.where(here, row.astype(F32), tag)
        slots[s][:, :width] = slot
        slots[s][:, width:] = tag.astype(BF16)


def attend_kernel(owners, bias, keys, values, *rest):
    slots, outs = rest[:owners], rest[owners:]
    users_here, _, width = keys.shape
    heads = bias.shape[0]
    size = width // heads
    scale = size ** (-0.5)
    for s in range(owners):
        tag = jnp.max(slots[s][:, width:].astype(F32))
        row = jnp.clip(tag.astype(jnp.int32), 0, users_here - 1)
        parts = []
        for h in range(heads):
            cut = slice(h * size, (h + 1) * size)
            logits = lax.dot_general(
                slots[s][:, cut],
                keys[row, :, cut],
                (((1,), (1,)), ((), ())),
                preferred_element_type=F32,
            )
            weight = silu(logits * scale + bias[h : h + 1, :]).astype(BF16)
            parts.append(jnp.dot(weight, values[row, :, cut], preferred_element_type=F32))
        mixture = jnp.concatenate(parts, axis=1)
        mean = jnp.mean(mixture, axis=1, keepdims=True)
        outs[s][:, :width] = (mixture - mean).astype(BF16)
        outs[s][:, width:] = in_lanes(split3(mean), MOST).astype(BF16)


def gate_kernel(candidates, weights, out_weight, w_score, gate_out, base_out, x, w, x_sems, w_sem):
    blocks = candidates.shape[0]
    rows = blocks * MOST
    width = w.shape[1]
    w_copy = pltpu.make_async_copy(weights.at[1], w, w_sem)
    w_copy.start()
    x_copies = [
        pltpu.make_async_copy(
            candidates.at[b, pl.ds(0, MOST)], x.at[pl.ds(b * MOST, MOST)], x_sems.at[b]
        )
        for b in range(blocks)
    ]
    for copy in x_copies:
        copy.start()
    for copy in x_copies:
        copy.wait()
    w_copy.wait()
    gate = silu(jnp.dot(x[...], w[...], preferred_element_type=F32))
    gate_out[...] = gate
    base_out[:rows, :] = jnp.dot(gate.astype(BF16), out_weight[...], preferred_element_type=F32)
    base_out[rows:, :] = jnp.zeros((base_out.shape[0] - rows, base_out.shape[1]), F32)
    base_out[rows : rows + 1, :width] = w_score[...]


def product_kernel(owners, users_here, block_user, own_map, me, gate, out_weight, *rest):
    slots = rest[:owners]
    full, sent = rest[owners:]
    width = gate.shape[1]
    model = out_weight.shape[1]
    blocks = gate.shape[0] // MOST
    centred, tails = [], []
    for b in range(blocks):
        owner, _ = placed(block_user, own_map, b, users_here)
        picked = slots[0][...]
        for s in range(1, owners):
            picked = jnp.where((owner ^ me[0]) == s, slots[s][...], picked)
        picked = picked.astype(F32)
        centred.append(picked[:, :width])
        tails.append(picked[:, width:])
    centred = jnp.concatenate(centred, axis=0)
    mean = joined(jnp.concatenate(tails, axis=0), 0)
    squares = jnp.sum(centred * centred, axis=1, keepdims=True)
    product = jnp.dot(
        (centred * gate[...]).astype(BF16), out_weight[...], preferred_element_type=F32
    )
    tail = in_lanes(split3(mean) + split3(squares), centred.shape[0])
    full[:, :model] = product
    full[:, model:] = tail
    sent[:, :model] = product.astype(BF16)
    sent[:, model:] = tail.astype(BF16)


def score_kernel(parts, block_count, me, candidates, *rest):
    bases, products, out = rest[:parts], rest[parts : 2 * parts], rest[2 * parts]
    x, sems = rest[2 * parts + 1 :]
    blocks, block_rows, model = candidates.shape
    rows = blocks * MOST
    width = model // parts
    copies = [
        pltpu.make_async_copy(
            candidates.at[b, pl.ds(0, MOST)], x.at[pl.ds(b * MOST, MOST)], sems.at[b]
        )
        for b in range(blocks)
    ]
    for copy in copies:
        copy.start()
    for copy in copies:
        copy.wait()
    tails = [p[:, model:].astype(F32) for p in products]
    means = [joined(t, 0) for t in tails]
    squares = sum(joined(t, 3) for t in tails)
    mean = sum(means) / parts
    spread = squares / model + sum((m - mean) * (m - mean) for m in means) / parts
    scale = lax.rsqrt(spread + EPSILON)
    total = sum(p[:, :model].astype(F32) for p in products)
    for m, base in zip(means, bases):
        total = total + (m - mean) * base[:rows, :]
    terms = silu(x[...].astype(F32) + total * scale)
    score = jnp.zeros((rows, 1), F32)
    for c in range(parts):
        vector = jnp.zeros((1, width), F32)
        for s in range(parts):
            vector = jnp.where((me[0] ^ s) == c, bases[s][rows : rows + 1, :width], vector)
        score = score + jnp.sum(
            terms[:, c * width : (c + 1) * width] * vector, axis=1, keepdims=True
        )
    place = lax.broadcasted_iota(jnp.int32, (MOST, block_rows), 0)
    lane = lax.broadcasted_iota(jnp.int32, (MOST, block_rows), 1)
    for b in range(blocks):
        keep = (place == lane) & (lane < block_count[b])
        spread_out = jnp.where(keep, score[b * MOST : (b + 1) * MOST], 0.0)
        out[b : b + 1, :] = jnp.sum(spread_out, axis=0, keepdims=True)


def exchange(arrays, axis):
    size = lax.axis_size(axis)
    return [arrays[0]] + [
        lax.ppermute(arrays[s], axis, [(k, k ^ s) for k in range(size)]) for s in range(1, size)
    ]


def local(
    candidates,
    block_user,
    block_count,
    own_map,
    history_key_cache,
    cache_values,
    w_query_unit,
    time_bias,
    output_weight,
    w_score,
):
    owners = lax.axis_size("users")
    parts = lax.axis_size("mp")
    user_index = lax.axis_index("users").astype(jnp.int32).reshape(1)
    model_index = lax.axis_index("mp").astype(jnp.int32).reshape(1)
    blocks, block_rows, model = candidates.shape
    users_here, _, width = history_key_cache.shape
    rows = blocks * MOST
    shape = jax.ShapeDtypeStruct

    def call(kernel, out_shape, in_specs, scratch=()):
        many = isinstance(out_shape, list)
        return pl.pallas_call(
            kernel,
            out_shape=out_shape,
            in_specs=in_specs,
            out_specs=[VMEM] * len(out_shape) if many else VMEM,
            scratch_shapes=list(scratch),
            compiler_params=pltpu.CompilerParams(vmem_limit_bytes=40 * 1024 * 1024),
        )

    loads = [
        pltpu.VMEM((rows, model), BF16),
        pltpu.VMEM((model, width), BF16),
        pltpu.SemaphoreType.DMA((blocks,)),
        pltpu.SemaphoreType.DMA,
    ]
    slots = call(
        functools.partial(query_kernel, owners, users_here),
        [shape((MOST, width + LANES), BF16)] * owners,
        [SMEM, SMEM, SMEM, ANY, ANY],
        loads,
    )(block_user, own_map, user_index, candidates, w_query_unit)
    slots = exchange(slots, "users")
    gate, base = call(
        gate_kernel,
        [shape((rows, width), F32), shape((rows + 8, model), F32)],
        [ANY, ANY, VMEM, VMEM],
        loads,
    )(candidates, w_query_unit, output_weight, w_score.reshape(1, width))
    bases = exchange([base] * parts, "mp")
    mixtures = call(
        functools.partial(attend_kernel, owners),
        [shape((MOST, width + LANES), BF16)] * owners,
        [VMEM] * (3 + owners),
    )(time_bias, history_key_cache, cache_values, *slots)
    mixtures = exchange(mixtures, "users")
    product, sent = call(
        functools.partial(product_kernel, owners, users_here),
        [shape((rows, model + LANES), F32), shape((rows, model + LANES), BF16)],
        [SMEM, SMEM, SMEM] + [VMEM] * (2 + owners),
    )(block_user, own_map, user_index, gate, output_weight, *mixtures)
    products = [product] + exchange([sent] * parts, "mp")[1:]
    return call(
        functools.partial(score_kernel, parts),
        shape((blocks, block_rows), F32),
        [SMEM, SMEM, ANY] + [VMEM] * (2 * parts),
        [pltpu.VMEM((rows, model), BF16), pltpu.SemaphoreType.DMA((blocks,))],
    )(block_count, model_index, candidates, *bases, *products)


def solution(mesh):
    return jax.shard_map(
        local,
        mesh=mesh,
        in_specs=(
            P(("groups", "users", "helpers"), None, None),
            P(("groups", "users", "helpers")),
            P(("groups", "users", "helpers")),
            P("groups"),
            P(("groups", "users"), None, "mp"),
            P(("groups", "users"), None, "mp"),
            P(None, None, "mp"),
            P("mp", None),
            P("mp", None),
            P("mp"),
        ),
        out_specs=P(("groups", "users", "helpers"), None),
        check_vma=False,
    )
```

```python
import functools

import jax
import jax.numpy as jnp
from jax import lax
from jax.experimental import pallas as pl
from jax.experimental.pallas import tpu as pltpu
from jax.sharding import PartitionSpec as P

EPSILON = 1e-05
MOST = 32
LANES = 128
F32 = jnp.float32
BF16 = jnp.bfloat16
VMEM = pl.BlockSpec(memory_space=pltpu.VMEM)
SMEM = pl.BlockSpec(memory_space=pltpu.SMEM)
HBM = pl.BlockSpec(memory_space=pltpu.HBM)


def silu(v):
    return v / (1.0 + jnp.exp(-v))


def split3(v):
    high = v.astype(BF16).astype(F32)
    rest = v - high
    middle = rest.astype(BF16).astype(F32)
    return high, middle, rest - middle


def in_lanes(columns, rows):
    lane = lax.broadcasted_iota(jnp.int32, (rows, LANES), 1)
    tail = jnp.zeros((rows, LANES), F32)
    for position, column in enumerate(columns):
        tail = jnp.where(lane == position, column, tail)
    return tail


def joined(tail, first):
    return tail[:, first : first + 1] + tail[:, first + 1 : first + 2] + tail[:, first + 2 : first + 3]


def placed(block_user, own_map, block, users_here):
    storage = own_map[block_user[block]]
    return storage // users_here, storage % users_here


def query_kernel(
    owners, users_here, user_source, map_source, count_source, me, candidates, weights, *rest
):
    slots, (x, place, counts) = rest[:owners], rest[owners : owners + 3]
    w, block_user, own_map, x_sems, sems = rest[owners + 3 :]
    blocks = candidates.shape[0]
    width = w.shape[1]
    w_copy = pltpu.make_async_copy(weights.at[0], w, sems.at[0])
    x_copies = [
        pltpu.make_async_copy(
            candidates.at[b, pl.ds(0, MOST)], x.at[pl.ds(b * MOST, MOST)], x_sems.at[b]
        )
        for b in range(blocks)
    ]
    small = [
        pltpu.make_async_copy(user_source, block_user, sems.at[1]),
        pltpu.make_async_copy(map_source, own_map, sems.at[2]),
        pltpu.make_async_copy(count_source, counts, sems.at[3]),
    ]
    for copy in small + x_copies + [w_copy]:
        copy.start()
    for copy in small:
        copy.wait()
    homes = [placed(block_user, own_map, b, users_here) for b in range(blocks)]
    for b, (owner, _) in enumerate(homes):
        place[b] = owner ^ me[0]
    for copy in x_copies + [w_copy]:
        copy.wait()
    query = silu(jnp.dot(x[...], w[...], preferred_element_type=F32)).astype(BF16)
    for s in range(owners):
        slot = jnp.zeros((MOST, width), BF16)
        tag = jnp.zeros((MOST, LANES), F32)
        for b, (owner, row) in enumerate(homes):
            here = (owner ^ me[0]) == s
            slot = jnp.where(here, query[b * MOST : (b + 1) * MOST], slot)
            tag = jnp.where(here, row.astype(F32), tag)
        slots[s][:, :width] = slot
        slots[s][:, width:] = tag.astype(BF16)


def attend_kernel(owners, _, bias, keys, values, *rest):
    slots, outs = rest[:owners], rest[owners : 2 * owners]
    v, v_sems = rest[2 * owners :]
    users_here, _, width = keys.shape
    heads = bias.shape[0]
    size = width // heads
    scale = size ** (-0.5)
    rows, copies = [], []
    for s in range(owners):
        tag = jnp.max(slots[s][:, width:].astype(F32))
        row = jnp.clip(tag.astype(jnp.int32), 0, users_here - 1)
        copy = pltpu.make_async_copy(values.at[row], v.at[s], v_sems.at[s])
        copy.start()
        rows.append(row)
        copies.append(copy)
    for s in range(owners):
        weights = []
        for h in range(heads):
            cut = slice(h * size, (h + 1) * size)
            logits = lax.dot_general(
                slots[s][:, cut],
                keys[rows[s], :, cut],
                (((1,), (1,)), ((), ())),
                preferred_element_type=F32,
            )
            weights.append(silu(logits * scale + bias[h : h + 1, :]).astype(BF16))
        copies[s].wait()
        parts = [
            jnp.dot(w, v[s, :, h * size : (h + 1) * size], preferred_element_type=F32)
            for h, w in enumerate(weights)
        ]
        mixture = jnp.concatenate(parts, axis=1)
        mean = jnp.mean(mixture, axis=1, keepdims=True)
        outs[s][:, :width] = (mixture - mean).astype(BF16)
        outs[s][:, width:] = in_lanes(split3(mean), MOST).astype(BF16)


def gate_kernel(_, x, weights, out_source, score_source, gate_out, base_out, out_w, w, vector, sems):
    rows = x.shape[0]
    width = w.shape[1]
    copies = [
        pltpu.make_async_copy(weights.at[1], w, sems.at[0]),
        pltpu.make_async_copy(out_source, out_w, sems.at[1]),
        pltpu.make_async_copy(score_source, vector, sems.at[2]),
    ]
    for copy in copies:
        copy.start()
    for copy in copies:
        copy.wait()
    gate = silu(jnp.dot(x[...], w[...], preferred_element_type=F32))
    gate_out[...] = gate
    base = jnp.dot(gate.astype(BF16), out_w[...], preferred_element_type=F32)
    base_out[:rows, :] = base.astype(BF16)
    line = lax.broadcasted_iota(jnp.int32, (16, width), 0)
    block = jnp.zeros((16, width), F32)
    for position, piece in enumerate(split3(vector[...])):
        block = jnp.where(line == position, piece, block)
    base_out[rows:, :] = jnp.zeros((16, base_out.shape[1]), BF16)
    base_out[rows:, :width] = block.astype(BF16)


def product_kernel(owners, place, gate, out_weight, *rest):
    slots = rest[:owners]
    full, sent = rest[owners:]
    width = gate.shape[1]
    model = out_weight.shape[1]
    blocks = gate.shape[0] // MOST
    centred, tails = [], []
    for b in range(blocks):
        picked = slots[0][...]
        for s in range(1, owners):
            picked = jnp.where(place[b] == s, slots[s][...], picked)
        picked = picked.astype(F32)
        centred.append(picked[:, :width])
        tails.append(picked[:, width:])
    centred = jnp.concatenate(centred, axis=0)
    mean = joined(jnp.concatenate(tails, axis=0), 0)
    squares = jnp.sum(centred * centred, axis=1, keepdims=True)
    product = jnp.dot(
        (centred * gate[...]).astype(BF16), out_weight[...], preferred_element_type=F32
    )
    tail = in_lanes(split3(mean) + split3(squares), centred.shape[0])
    full[:, :model] = product
    full[:, model:] = tail
    sent[:, :model] = product.astype(BF16)
    sent[:, model:] = tail.astype(BF16)


def score_kernel(parts, block_count, me, x, *rest):
    bases, products, out = rest[:parts], rest[parts : 2 * parts], rest[2 * parts]
    blocks, block_rows = out.shape
    rows, model = x.shape
    width = model // parts
    tails = [p[:, model:].astype(F32) for p in products]
    means = [joined(t, 0) for t in tails]
    squares = sum(joined(t, 3) for t in tails)
    mean = sum(means) / parts
    spread = squares / model + sum((m - mean) * (m - mean) for m in means) / parts
    scale = lax.rsqrt(spread + EPSILON)
    total = sum(p[:, :model].astype(F32) for p in products)
    for m, base in zip(means, bases):
        total = total + (m - mean) * base[:rows, :].astype(F32)
    terms = silu(x[...].astype(F32) + total * scale)
    score = jnp.zeros((rows, 1), F32)
    for c in range(parts):
        vector = jnp.zeros((1, width), F32)
        for s in range(parts):
            pieces = bases[s][rows:, :width].astype(F32)
            whole = pieces[0:1] + pieces[1:2] + pieces[2:3]
            vector = jnp.where((me[0] ^ s) == c, whole, vector)
        score = score + jnp.sum(
            terms[:, c * width : (c + 1) * width] * vector, axis=1, keepdims=True
        )
    place = lax.broadcasted_iota(jnp.int32, (MOST, block_rows), 0)
    lane = lax.broadcasted_iota(jnp.int32, (MOST, block_rows), 1)
    for b in range(blocks):
        keep = (place == lane) & (lane < block_count[b])
        spread_out = jnp.where(keep, score[b * MOST : (b + 1) * MOST], 0.0)
        out[b : b + 1, :] = jnp.sum(spread_out, axis=0, keepdims=True)


def exchange(arrays, axis):
    size = lax.axis_size(axis)
    return [arrays[0]] + [
        lax.ppermute(arrays[s], axis, [(k, k ^ s) for k in range(size)]) for s in range(1, size)
    ]


def local(
    candidates,
    block_user,
    block_count,
    own_map,
    history_key_cache,
    cache_values,
    w_query_unit,
    time_bias,
    output_weight,
    w_score,
):
    owners = lax.axis_size("users")
    parts = lax.axis_size("mp")
    user_index = lax.axis_index("users").astype(jnp.int32).reshape(1)
    model_index = lax.axis_index("mp").astype(jnp.int32).reshape(1)
    blocks, block_rows, model = candidates.shape
    users_here, _, width = history_key_cache.shape
    rows = blocks * MOST
    shape = jax.ShapeDtypeStruct

    def call(kernel, out_shape, in_specs, out_specs, scratch=()):
        return pl.pallas_call(
            kernel,
            out_shape=out_shape,
            in_specs=in_specs,
            out_specs=out_specs,
            scratch_shapes=list(scratch),
            compiler_params=pltpu.CompilerParams(vmem_limit_bytes=8 * 1024 * 1024),
        )

    block_user, own_map, block_count, candidates, w_query_unit, output_weight, score_row, value_cache = (
        pltpu.with_memory_space_constraint(a, pltpu.HBM)
        for a in (
            block_user, own_map, block_count, candidates, w_query_unit, output_weight, w_score.reshape(1, width), cache_values,
        )
    )
    slot = shape((MOST, width + LANES), BF16)
    numbers = shape((blocks,), jnp.int32)
    *slots, x, place, counts = call(
        functools.partial(query_kernel, owners, users_here),
        [slot] * owners + [shape((rows, model), BF16), numbers, numbers],
        [HBM, HBM, HBM, SMEM, HBM, HBM],
        [VMEM] * (owners + 1) + [SMEM, SMEM],
        [
            pltpu.VMEM((model, width), BF16),
            pltpu.SMEM(block_user.shape, jnp.int32),
            pltpu.SMEM(own_map.shape, jnp.int32),
            pltpu.SemaphoreType.DMA((blocks,)),
            pltpu.SemaphoreType.DMA((4,)),
        ],
    )(block_user, own_map, block_count, user_index, candidates, w_query_unit)
    slots = exchange(slots, "users")
    gate, base, out_w = call(
        gate_kernel,
        [
            shape((rows, width), F32),
            shape((rows + 16, model), BF16),
            shape(output_weight.shape, BF16),
        ],
        [VMEM, VMEM, HBM, HBM, HBM],
        [VMEM] * 3,
        [
            pltpu.VMEM((model, width), BF16),
            pltpu.VMEM((1, width), F32),
            pltpu.SemaphoreType.DMA((3,)),
        ],
    )(slots[1], x, w_query_unit, output_weight, score_row)
    bases = exchange([base] * parts, "mp")
    mixtures = call(
        functools.partial(attend_kernel, owners),
        [slot] * owners,
        [VMEM, VMEM, VMEM, HBM] + [VMEM] * owners,
        [VMEM] * owners,
        [
            pltpu.VMEM((owners, *history_key_cache.shape[1:]), BF16),
            pltpu.SemaphoreType.DMA((owners,)),
        ],
    )(gate, time_bias, history_key_cache, value_cache, *slots)
    mixtures = exchange(mixtures, "users")
    product, sent = call(
        functools.partial(product_kernel, owners),
        [shape((rows, model + LANES), F32), shape((rows, model + LANES), BF16)],
        [SMEM] + [VMEM] * (2 + owners),
        [VMEM] * 2,
    )(place, gate, out_w, *mixtures)
    products = [product] + exchange([sent] * parts, "mp")[1:]
    return call(
        functools.partial(score_kernel, parts),
        shape((blocks, block_rows), F32),
        [SMEM, SMEM] + [VMEM] * (1 + 2 * parts),
        VMEM,
    )(counts, model_index, x, *bases, *products)


def solution(mesh):
    return jax.shard_map(
        local,
        mesh=mesh,
        in_specs=(
            P(("groups", "users", "helpers"), None, None),
            P(("groups", "users", "helpers")),
            P(("groups", "users", "helpers")),
            P("groups"),
            P(("groups", "users"), None, "mp"),
            P(("groups", "users"), None, "mp"),
            P(None, None, "mp"),
            P("mp", None),
            P("mp", None),
            P("mp"),
        ),
        out_specs=P(("groups", "users", "helpers"), None),
        check_vma=False,
    )
```

```python
import functools

import jax
import jax.numpy as jnp
from jax import lax
from jax.experimental import pallas as pl
from jax.experimental.pallas import tpu as pltpu
from jax.sharding import PartitionSpec as P

EPSILON = 1e-05
MOST = 32
LANES = 128
TAIL = 16
CHUNKS = 4
F32 = jnp.float32
BF16 = jnp.bfloat16
VMEM = pl.BlockSpec(memory_space=pltpu.VMEM)
HBM = pl.BlockSpec(memory_space=pltpu.HBM)


def silu(v):
    return v / (1.0 + jnp.exp(-v))


def split3(v):
    high = v.astype(BF16).astype(F32)
    rest = v - high
    middle = rest.astype(BF16).astype(F32)
    return high, middle, rest - middle


def in_lanes(columns, rows):
    lane = lax.broadcasted_iota(jnp.int32, (rows, LANES), 1)
    tail = jnp.zeros((rows, LANES), F32)
    for position, column in enumerate(columns):
        tail = jnp.where(lane == position, column, tail)
    return tail


def joined(tail, first):
    return tail[:, first : first + 1] + tail[:, first + 1 : first + 2] + tail[:, first + 2 : first + 3]


def diagonal(width):
    row = lax.broadcasted_iota(jnp.int32, (MOST, width), 0)
    return row == lax.broadcasted_iota(jnp.int32, (MOST, width), 1)


def query_kernel(owners, users_here, heads, user_source, map_source, candidates, weights, *rest):
    slots, (x, notes) = rest[:owners], rest[owners : owners + 2]
    w, block_user, own_map, x_sems, w_sems, sems = rest[owners + 2 :]
    blocks = candidates.shape[0]
    model, width = w.shape
    size = width // heads
    part = model // CHUNKS
    small = [
        pltpu.make_async_copy(user_source, block_user, sems.at[0]),
        pltpu.make_async_copy(map_source, own_map, sems.at[1]),
    ]
    x_copies = [
        pltpu.make_async_copy(
            candidates.at[b, pl.ds(0, MOST)], x.at[pl.ds(b * MOST, MOST)], x_sems.at[b]
        )
        for b in range(blocks)
    ]
    w_copies = [
        pltpu.make_async_copy(
            weights.at[0, pl.ds(i * part, part)], w.at[pl.ds(i * part, part)], w_sems.at[i]
        )
        for i in range(CHUNKS)
    ]
    for copy in small + x_copies + w_copies:
        copy.start()
    for copy in small:
        copy.wait()
    me = lax.axis_index("users")
    homes = []
    for b in range(blocks):
        storage = own_map[block_user[b]]
        homes.append(((storage // users_here) ^ me, storage % users_here))
        notes[b : b + 1, :] = jnp.full((1, LANES), homes[b][0], jnp.int32)
    for copy in x_copies:
        copy.wait()
    query = jnp.zeros((blocks * MOST, width), F32)
    for i, copy in enumerate(w_copies):
        copy.wait()
        cut = slice(i * part, (i + 1) * part)
        query += jnp.dot(x[:, cut], w[cut, :], preferred_element_type=F32)
    query = silu(query).astype(BF16)
    for s in range(owners):
        tag = jnp.zeros((TAIL, size), F32)
        for b, (slot, row) in enumerate(homes):
            tag = jnp.where(slot == s, row.astype(F32), tag)
        for h in range(heads):
            piece = jnp.zeros((MOST, size), BF16)
            for b, (slot, row) in enumerate(homes):
                mine = query[b * MOST : (b + 1) * MOST, h * size : (h + 1) * size]
                piece = jnp.where(slot == s, mine, piece)
            slots[s][h * MOST : (h + 1) * MOST, :] = piece
        slots[s][heads * MOST :, :] = tag.astype(BF16)


def attend_kernel(owners, _, bias, keys, values, *rest):
    slots, outs = rest[:owners][::-1], rest[owners : 2 * owners]
    v, v_sems = rest[2 * owners :]
    users_here, _, width = keys.shape
    heads = bias.shape[0]
    size = width // heads
    scale = size ** (-0.5)
    rows, copies, weights = [], [], []
    for s in range(owners):
        tag = jnp.max(slots[s][heads * MOST :, :].astype(F32))
        row = jnp.clip(tag.astype(jnp.int32), 0, users_here - 1)
        copy = pltpu.make_async_copy(values.at[row], v.at[s], v_sems.at[s])
        copy.start()
        rows.append(row)
        copies.append(copy)
    for s in range(owners):
        for h in range(heads):
            logits = lax.dot_general(
                slots[s][h * MOST : (h + 1) * MOST, :],
                keys[rows[s], :, h * size : (h + 1) * size],
                (((1,), (1,)), ((), ())),
                preferred_element_type=F32,
            )
            weights.append(silu(logits * scale + bias[h : h + 1, :]).astype(BF16))
    mask = diagonal(size)
    for s in range(owners):
        copies[s].wait()
        parts = [
            jnp.dot(
                weights[s * heads + h],
                v[s, :, h * size : (h + 1) * size],
                preferred_element_type=F32,
            )
            for h in range(heads)
        ]
        mean = jnp.sum(sum(parts), axis=1, keepdims=True) / width
        mean = mean.astype(BF16).astype(F32)
        for h, part in enumerate(parts):
            outs[s][h * MOST : (h + 1) * MOST, :] = (part - mean).astype(BF16)
        line = jnp.sum(jnp.where(mask, mean, 0.0), axis=0, keepdims=True)
        outs[s][heads * MOST :, :] = jnp.broadcast_to(line, (TAIL, size)).astype(BF16)


def gate_kernel(
    x, weights, out_source, score_source, count_source, gate_out, base_out, out_w, counts, *rest
):
    w, vector, block_count, sems = rest
    rows = x.shape[0]
    width = w.shape[1]
    model = base_out.shape[1]
    copies = [
        pltpu.make_async_copy(count_source, block_count, sems.at[3]),
        pltpu.make_async_copy(score_source, vector, sems.at[2]),
        pltpu.make_async_copy(weights.at[1], w, sems.at[0]),
        pltpu.make_async_copy(out_source, out_w, sems.at[1]),
    ]
    for copy in copies:
        copy.start()
    copies[0].wait()
    for b in range(block_count.shape[0]):
        counts[b : b + 1, :] = jnp.full((1, LANES), block_count[b], jnp.int32)
    copies[1].wait()
    line = lax.broadcasted_iota(jnp.int32, (TAIL, width), 0)
    block = jnp.zeros((TAIL, width), F32)
    for position, piece in enumerate(split3(vector[...])):
        block = jnp.where(line == position, piece, block)
    block = block.astype(BF16)
    me = lax.axis_index("mp")
    for c in range(model // width):
        base_out[rows:, c * width : (c + 1) * width] = jnp.where(
            me == c, block, jnp.zeros_like(block)
        )
    copies[2].wait()
    gate = silu(jnp.dot(x[...], w[...], preferred_element_type=F32))
    gate_out[...] = gate
    copies[3].wait()
    base = jnp.dot(gate.astype(BF16), out_w[...], preferred_element_type=F32)
    base_out[:rows, :] = base.astype(BF16)


def product_kernel(owners, notes, gate, out_weight, *rest):
    slots = rest[:owners][::-1]
    full, sent = rest[owners:]
    width = gate.shape[1]
    model = out_weight.shape[1]
    blocks = gate.shape[0] // MOST
    size = slots[0].shape[1]
    heads = width // size
    mask = diagonal(size)
    means, squares, gated = [], [], []
    for b in range(blocks):
        place = notes[b : b + 1, :size]
        picked = slots[0][...].astype(F32)
        for s in range(1, owners):
            picked = jnp.where(place == s, slots[s][...].astype(F32), picked)
        parts = [picked[h * MOST : (h + 1) * MOST] for h in range(heads)]
        extra = jnp.sum(sum(parts), axis=1, keepdims=True) / width
        base = jnp.sum(
            jnp.where(mask, picked[heads * MOST : heads * MOST + 1], 0.0), axis=1, keepdims=True
        )
        parts = [part - extra for part in parts]
        means.append(base + extra)
        squares.append(jnp.sum(sum(part * part for part in parts), axis=1, keepdims=True))
        gated.append(
            jnp.concatenate(
                [
                    part * gate[b * MOST : (b + 1) * MOST, h * size : (h + 1) * size]
                    for h, part in enumerate(parts)
                ],
                axis=1,
            )
        )
    mean = jnp.concatenate(means, axis=0)
    square = jnp.concatenate(squares, axis=0)
    product = jnp.dot(
        jnp.concatenate(gated, axis=0).astype(BF16), out_weight[...], preferred_element_type=F32
    )
    tail = in_lanes(split3(mean) + split3(square), mean.shape[0])
    full[:, :model] = product
    full[:, model:] = tail
    sent[:, :model] = product.astype(BF16)
    sent[:, model:] = tail.astype(BF16)


def score_kernel(parts, counts, x, *rest):
    bases, products, out = rest[:parts], rest[parts : 2 * parts], rest[2 * parts]
    blocks, block_rows = out.shape
    rows, model = x.shape
    tails = [p[:, model:].astype(F32) for p in products]
    means = [joined(t, 0) for t in tails]
    squares = sum(joined(t, 3) for t in tails)
    mean = sum(means) / parts
    spread = squares / model + sum((m - mean) * (m - mean) for m in means) / parts
    scale = lax.rsqrt(spread + EPSILON)
    total = sum(p[:, :model].astype(F32) for p in products)
    for m, base in zip(means, bases):
        total = total + (m - mean) * base[:rows, :].astype(F32)
    terms = silu(x[...].astype(F32) + total * scale)
    pieces = sum(base[rows:, :].astype(F32) for base in bases)
    vector = pieces[0:1] + pieces[1:2] + pieces[2:3]
    score = jnp.sum(terms * vector, axis=1, keepdims=True)
    mask = diagonal(block_rows)
    lane = lax.broadcasted_iota(jnp.int32, (1, block_rows), 1)
    for b in range(blocks):
        line = jnp.sum(
            jnp.where(mask, score[b * MOST : (b + 1) * MOST], 0.0), axis=0, keepdims=True
        )
        out[b : b + 1, :] = jnp.where(lane < counts[b : b + 1, :block_rows], line, 0.0)


def swap(arrays, axis, cross=None):
    size = lax.axis_size(axis)
    out = [None] * size
    out[0] = arrays[0]
    for s in range(size - 1, 0, -1):
        if cross is None:
            out[s] = lax.ppermute(arrays[s], axis, [(k, k ^ s) for k in range(size)])
        else:
            cores = lax.axis_size(cross)
            pairs = [
                (k * cores + c, (k ^ s) * cores + cores - 1 - c)
                for k in range(size)
                for c in range(cores)
            ]
            out[s] = lax.ppermute(arrays[s], (axis, cross), pairs)
    return out


def local(
    candidates,
    block_user,
    block_count,
    own_map,
    history_key_cache,
    cache_values,
    w_query_unit,
    time_bias,
    output_weight,
    w_score,
):
    owners = lax.axis_size("users")
    parts = lax.axis_size("mp")
    blocks, block_rows, model = candidates.shape
    users_here, _, width = history_key_cache.shape
    rows = blocks * MOST
    shape = jax.ShapeDtypeStruct

    def call(kernel, out_shape, in_specs, out_specs, scratch=()):
        return pl.pallas_call(
            kernel,
            out_shape=out_shape,
            in_specs=in_specs,
            out_specs=out_specs,
            scratch_shapes=list(scratch),
            compiler_params=pltpu.CompilerParams(vmem_limit_bytes=8 * 1024 * 1024),
        )

    block_user, own_map, block_count, candidates, w_query_unit, output_weight, score_row, value_cache = (
        pltpu.with_memory_space_constraint(a, pltpu.HBM)
        for a in (
            block_user, own_map, block_count, candidates, w_query_unit, output_weight, w_score.reshape(1, width), cache_values,
        )
    )
    heads = time_bias.shape[0]
    slot = shape((heads * MOST + TAIL, width // heads), BF16)
    notes_shape = shape((blocks, LANES), jnp.int32)
    *slots, x, notes = call(
        functools.partial(query_kernel, owners, users_here, heads),
        [slot] * owners + [shape((rows, model), BF16), notes_shape],
        [HBM] * 4,
        [VMEM] * (owners + 2),
        [
            pltpu.VMEM((model, width), BF16),
            pltpu.SMEM(block_user.shape, jnp.int32),
            pltpu.SMEM(own_map.shape, jnp.int32),
            pltpu.SemaphoreType.DMA((blocks,)),
            pltpu.SemaphoreType.DMA((CHUNKS,)),
            pltpu.SemaphoreType.DMA((2,)),
        ],
    )(block_user, own_map, candidates, w_query_unit)
    slots = swap(slots, "users", "helpers")
    gate, base, out_w, counts = call(
        gate_kernel,
        [
            shape((rows, width), F32),
            shape((rows + TAIL, model), BF16),
            shape(output_weight.shape, BF16),
            notes_shape,
        ],
        [VMEM, HBM, HBM, HBM, HBM],
        [VMEM] * 4,
        [
            pltpu.VMEM((model, width), BF16),
            pltpu.VMEM((1, width), F32),
            pltpu.SMEM(block_count.shape, jnp.int32),
            pltpu.SemaphoreType.DMA((4,)),
        ],
    )(x, w_query_unit, output_weight, score_row, block_count)
    bases = swap([base] * parts, "mp")
    mixtures = call(
        functools.partial(attend_kernel, owners),
        [slot] * owners,
        [VMEM, VMEM, VMEM, HBM] + [VMEM] * owners,
        [VMEM] * owners,
        [
            pltpu.VMEM((owners, *history_key_cache.shape[1:]), BF16),
            pltpu.SemaphoreType.DMA((owners,)),
        ],
    )(gate, time_bias, history_key_cache, value_cache, *slots[::-1])
    mixtures = swap(mixtures, "users", "helpers")
    product, sent = call(
        functools.partial(product_kernel, owners),
        [shape((rows, model + LANES), F32), shape((rows, model + LANES), BF16)],
        [VMEM] * (3 + owners),
        [VMEM] * 2,
    )(notes, gate, out_w, *mixtures[::-1])
    products = [product] + swap([sent] * parts, "mp")[1:]
    return call(
        functools.partial(score_kernel, parts),
        shape((blocks, block_rows), F32),
        [VMEM] * (2 + 2 * parts),
        VMEM,
    )(counts, x, *bases, *products)


def solution(mesh):
    return jax.shard_map(
        local,
        mesh=mesh,
        in_specs=(
            P(("groups", "users", "helpers"), None, None),
            P(("groups", "users", "helpers")),
            P(("groups", "users", "helpers")),
            P("groups"),
            P(("groups", "users"), None, "mp"),
            P(("groups", "users"), None, "mp"),
            P(None, None, "mp"),
            P("mp", None),
            P("mp", None),
            P("mp"),
        ),
        out_specs=P(("groups", "users", "helpers"), None),
        check_vma=False,
    )
```

```python
import functools

import jax
import jax.numpy as jnp
from jax import lax
from jax.experimental import pallas as pl
from jax.experimental.pallas import tpu as pltpu
from jax.sharding import PartitionSpec as P

EPSILON = 1e-05
MOST = 32
LANES = 128
TAIL = 16
CHUNKS = 4
F32 = jnp.float32
BF16 = jnp.bfloat16
VMEM = pl.BlockSpec(memory_space=pltpu.VMEM)
HBM = pl.BlockSpec(memory_space=pltpu.HBM)


def silu(v):
    return v / (1.0 + jnp.exp(-v))


def split3(v):
    high = v.astype(BF16).astype(F32)
    rest = v - high
    middle = rest.astype(BF16).astype(F32)
    return high, middle, rest - middle


def at_lane(shift):
    row = lax.broadcasted_iota(jnp.int32, (MOST, LANES), 0)
    return row + shift == lax.broadcasted_iota(jnp.int32, (MOST, LANES), 1)


def to_line(column, mask):
    return jnp.sum(jnp.where(mask, column, 0.0), axis=0, keepdims=True)


def to_column(line, mask):
    return jnp.sum(jnp.where(mask, line, 0.0), axis=1, keepdims=True)


def whole_tiles(rows):
    return -(-rows // TAIL) * TAIL


def query_kernel(owners, users_here, heads, user_source, map_source, candidates, weights, *rest):
    slots, (x, notes) = rest[:owners], rest[owners : owners + 2]
    w, block_user, own_map, x_sems, w_sems, sems = rest[owners + 2 :]
    blocks = candidates.shape[0]
    model, width = w.shape
    size = width // heads
    part = model // CHUNKS
    small = [
        pltpu.make_async_copy(user_source, block_user, sems.at[0]),
        pltpu.make_async_copy(map_source, own_map, sems.at[1]),
    ]
    x_copies = [
        pltpu.make_async_copy(
            candidates.at[b, pl.ds(0, MOST)], x.at[pl.ds(b * MOST, MOST)], x_sems.at[b]
        )
        for b in range(blocks)
    ]
    w_copies = [
        pltpu.make_async_copy(
            weights.at[0, pl.ds(i * part, part)], w.at[pl.ds(i * part, part)], w_sems.at[i]
        )
        for i in range(CHUNKS)
    ]
    for copy in small + x_copies + w_copies:
        copy.start()
    for copy in small:
        copy.wait()
    me = lax.axis_index("users")
    homes = []
    for b in range(blocks):
        storage = own_map[block_user[b]]
        homes.append(((storage // users_here) ^ me, storage % users_here))
        notes[b : b + 1, :] = jnp.full((1, LANES), homes[b][0], jnp.int32)
    for copy in x_copies:
        copy.wait()
    query = jnp.zeros((blocks * MOST, width), F32)
    for i, copy in enumerate(w_copies):
        copy.wait()
        cut = slice(i * part, (i + 1) * part)
        query += jnp.dot(x[:, cut], w[cut, :], preferred_element_type=F32)
    query = silu(query).astype(BF16)
    for s in range(owners):
        tag = jnp.zeros((TAIL, size), F32)
        for b, (slot, row) in enumerate(homes):
            tag = jnp.where(slot == s, row.astype(F32), tag)
        for h in range(heads):
            piece = jnp.zeros((MOST, size), BF16)
            for b, (slot, row) in enumerate(homes):
                mine = query[b * MOST : (b + 1) * MOST, h * size : (h + 1) * size]
                piece = jnp.where(slot == s, mine, piece)
            slots[s][h * MOST : (h + 1) * MOST, :] = piece
        slots[s][heads * MOST :, :] = tag.astype(BF16)


def attend_kernel(owners, bias, keys, values, *rest):
    slots, outs = rest[:owners][::-1], rest[owners : 2 * owners]
    users_here, history, width = keys.shape
    heads = bias.shape[0]
    size = width // heads
    scale = size ** (-0.5)
    rows, weights = [], []
    for s in range(owners):
        tag = jnp.max(slots[s][heads * MOST :, :].astype(F32))
        row = jnp.clip(tag.astype(jnp.int32), 0, users_here - 1)
        rows.append(row)
    none = jnp.zeros((MOST, size), BF16)
    for s in range(owners):
        for h in range(0, heads, 2):
            one = slots[s][h * MOST : (h + 1) * MOST, :]
            two = slots[s][(h + 1) * MOST : (h + 2) * MOST, :]
            query = jnp.concatenate(
                [jnp.concatenate([one, none], axis=1), jnp.concatenate([none, two], axis=1)], axis=0
            )
            logits = lax.dot_general(
                query,
                keys[rows[s], :, h * size : (h + 2) * size],
                (((1,), (1,)), ((), ())),
                preferred_element_type=F32,
            )
            pair = jnp.concatenate(
                [jnp.broadcast_to(bias[h + i : h + i + 1, :], (MOST, history)) for i in range(2)]
            )
            weights.append(silu(logits * scale + pair).astype(BF16))
    mask = at_lane(0)
    for s in range(owners):
        parts = []
        for h in range(0, heads, 2):
            mixed = jnp.dot(
                weights[(s * heads + h) // 2],
                values[rows[s], :, h * size : (h + 2) * size],
                preferred_element_type=F32,
            )
            parts += [mixed[:MOST, :size], mixed[MOST:, size:]]
        mean = jnp.sum(sum(parts), axis=1, keepdims=True) / width
        mean = mean.astype(BF16).astype(F32)
        for h, part in enumerate(parts):
            outs[s][h * MOST : (h + 1) * MOST, :] = (part - mean).astype(BF16)
        outs[s][heads * MOST :, :] = jnp.broadcast_to(to_line(mean, mask), (TAIL, size)).astype(BF16)


def gate_kernel(x, weights, out_source, score_source, count_source, value_source, *rest):
    gate_out, base_out, out_w, counts, values, w, vector, block_count, sems = rest
    rows = x.shape[0]
    width = w.shape[1]
    model = out_w.shape[1]
    copies = [
        pltpu.make_async_copy(count_source, block_count, sems.at[3]),
        pltpu.make_async_copy(score_source, vector, sems.at[2]),
        pltpu.make_async_copy(weights.at[1], w, sems.at[0]),
        pltpu.make_async_copy(out_source, out_w, sems.at[1]),
        pltpu.make_async_copy(value_source, values, sems.at[4]),
    ]
    for copy in copies:
        copy.start()
    copies[0].wait()
    for b in range(block_count.shape[0]):
        counts[b : b + 1, :] = jnp.full((1, LANES), block_count[b], jnp.int32)
    copies[1].wait()
    chunks = model // LANES
    pieces = jnp.concatenate(split3(vector[...]), axis=0).astype(BF16)
    base_out[chunks * rows :, :] = jnp.zeros((base_out.shape[0] - chunks * rows, LANES), BF16)
    base_out[chunks * rows : chunks * rows + pieces.shape[0], :] = pieces
    copies[2].wait()
    gate = silu(jnp.dot(x[...], w[...], preferred_element_type=F32))
    gate_out[...] = gate
    copies[3].wait()
    base = jnp.dot(gate.astype(BF16), out_w[...], preferred_element_type=F32)
    for c in range(chunks):
        base_out[c * rows : (c + 1) * rows, :] = base[:, c * LANES : (c + 1) * LANES].astype(BF16)
    copies[4].wait()


def product_kernel(owners, notes, gate, out_weight, *rest):
    slots = rest[:owners][::-1]
    full, sent = rest[owners:]
    rows, width = gate.shape
    chunks = out_weight.shape[1] // LANES
    blocks = rows // MOST
    size = slots[0].shape[1]
    heads = width // size
    group = LANES // MOST
    lines = [[jnp.zeros((1, LANES), F32)] * 6 for _ in range(-(-blocks // group))]
    gated = []
    for b in range(blocks):
        place = notes[b : b + 1, :size]
        picked = slots[0][...].astype(F32)
        for s in range(1, owners):
            picked = jnp.where(place == s, slots[s][...].astype(F32), picked)
        parts = [picked[h * MOST : (h + 1) * MOST] for h in range(heads)]
        extra = jnp.sum(sum(parts), axis=1, keepdims=True) / width
        mean = to_column(picked[heads * MOST : heads * MOST + 1], at_lane(0)) + extra
        parts = [part - extra for part in parts]
        square = jnp.sum(sum(part * part for part in parts), axis=1, keepdims=True)
        mask = at_lane(b % group * MOST)
        values = (*split3(to_line(mean, mask)), *split3(to_line(square, mask)))
        lines[b // group] = [one + two for one, two in zip(lines[b // group], values)]
        gated.append(
            jnp.concatenate(
                [
                    part * gate[b * MOST : (b + 1) * MOST, h * size : (h + 1) * size]
                    for h, part in enumerate(parts)
                ],
                axis=1,
            )
        )
    product = jnp.dot(
        jnp.concatenate(gated, axis=0).astype(BF16), out_weight[...], preferred_element_type=F32
    )
    tail = jnp.concatenate([line for part in lines for line in part], axis=0)
    for ref, kind in ((full, F32), (sent, BF16)):
        for c in range(chunks):
            ref[c * rows : (c + 1) * rows, :] = product[:, c * LANES : (c + 1) * LANES].astype(kind)
        ref[chunks * rows :, :] = jnp.zeros((ref.shape[0] - chunks * rows, LANES), kind)
        ref[chunks * rows : chunks * rows + tail.shape[0], :] = tail.astype(kind)


def score_kernel(parts, counts, x, *rest):
    bases, products, out = rest[:parts], rest[parts : 2 * parts], rest[2 * parts]
    blocks, block_rows = out.shape
    rows, model = x.shape
    chunks = model // LANES
    own = chunks // parts
    group = LANES // MOST
    means, squares = [], []
    for p in products:
        tail = p[chunks * rows :, :].astype(F32)
        mean, square = [], []
        for b in range(blocks):
            mask = at_lane(b % group * MOST)
            first = b // group * 6
            line = tail[first : first + 1] + tail[first + 1 : first + 2] + tail[first + 2 : first + 3]
            mean.append(to_column(line, mask))
            first += 3
            line = tail[first : first + 1] + tail[first + 1 : first + 2] + tail[first + 2 : first + 3]
            square.append(to_column(line, mask))
        means.append(jnp.concatenate(mean, axis=0))
        squares.append(jnp.concatenate(square, axis=0))
    mean = sum(means) / parts
    offsets = [m - mean for m in means]
    spread = sum(squares) / model + sum(d * d for d in offsets) / parts
    scale = lax.rsqrt(spread + EPSILON)
    me = lax.axis_index("mp")
    vectors = [base[chunks * rows : chunks * rows + 3 * own, :].astype(F32) for base in bases]
    vectors = [v[:own] + v[own : 2 * own] + v[2 * own :] for v in vectors]
    score = jnp.zeros((rows, LANES), F32)
    for c in range(chunks):
        cut = slice(c * rows, (c + 1) * rows)
        total = sum(p[cut, :].astype(F32) for p in products)
        for d, base in zip(offsets, bases):
            total = total + d * base[cut, :].astype(F32)
        vector = vectors[0][c % own : c % own + 1]
        for s in range(1, parts):
            vector = jnp.where((me ^ s) == c // own, vectors[s][c % own : c % own + 1], vector)
        feature = x[:, c * LANES : (c + 1) * LANES].astype(F32)
        score = score + silu(feature + total * scale) * vector
    score = jnp.sum(score, axis=1, keepdims=True)
    mask = at_lane(0)
    lane = lax.broadcasted_iota(jnp.int32, (1, LANES), 1)
    for b in range(blocks):
        line = to_line(score[b * MOST : (b + 1) * MOST], mask)
        line = jnp.where(lane < counts[b : b + 1, :], line, 0.0)
        out[b : b + 1, :LANES] = line
        if block_rows > LANES:
            out[b : b + 1, LANES:] = jnp.zeros((1, block_rows - LANES), F32)


def swap(arrays, axis, cross=None):
    size = lax.axis_size(axis)
    out = [None] * size
    out[0] = arrays[0]
    for s in range(size - 1, 0, -1):
        if cross is None:
            out[s] = lax.ppermute(arrays[s], axis, [(k, k ^ s) for k in range(size)])
        else:
            cores = lax.axis_size(cross)
            pairs = [
                (k * cores + c, (k ^ s) * cores + cores - 1 - c)
                for k in range(size)
                for c in range(cores)
            ]
            out[s] = lax.ppermute(arrays[s], (axis, cross), pairs)
    return out


def local(
    candidates,
    block_user,
    block_count,
    own_map,
    history_key_cache,
    cache_values,
    w_query_unit,
    time_bias,
    output_weight,
    w_score,
):
    owners = lax.axis_size("users")
    parts = lax.axis_size("mp")
    blocks, block_rows, model = candidates.shape
    users_here, _, width = history_key_cache.shape
    rows = blocks * MOST
    shape = jax.ShapeDtypeStruct

    def call(kernel, out_shape, in_specs, out_specs, scratch=()):
        return pl.pallas_call(
            kernel,
            out_shape=out_shape,
            in_specs=in_specs,
            out_specs=out_specs,
            scratch_shapes=list(scratch),
            compiler_params=pltpu.CompilerParams(vmem_limit_bytes=8 * 1024 * 1024),
        )

    block_user, own_map, block_count, candidates, w_query_unit, output_weight, score_row, value_cache = (
        pltpu.with_memory_space_constraint(a, pltpu.HBM)
        for a in (
            block_user, own_map, block_count, candidates, w_query_unit, output_weight, w_score.reshape(width // LANES, LANES), cache_values,
        )
    )
    heads = time_bias.shape[0]
    chunks = model // LANES
    sums = (chunks * rows + whole_tiles(6 * -(-rows // LANES)), LANES)
    slot = shape((heads * MOST + TAIL, width // heads), BF16)
    notes_shape = shape((blocks, LANES), jnp.int32)
    *slots, x, notes = call(
        functools.partial(query_kernel, owners, users_here, heads),
        [slot] * owners + [shape((rows, model), BF16), notes_shape],
        [HBM] * 4,
        [VMEM] * (owners + 2),
        [
            pltpu.VMEM((model, width), BF16),
            pltpu.SMEM(block_user.shape, jnp.int32),
            pltpu.SMEM(own_map.shape, jnp.int32),
            pltpu.SemaphoreType.DMA((blocks,)),
            pltpu.SemaphoreType.DMA((CHUNKS,)),
            pltpu.SemaphoreType.DMA((2,)),
        ],
    )(block_user, own_map, candidates, w_query_unit)
    slots = swap(slots, "users", "helpers")
    gate, base, out_w, counts, values = call(
        gate_kernel,
        [
            shape((rows, width), F32),
            shape((chunks * rows + whole_tiles(3 * width // LANES), LANES), BF16),
            shape(output_weight.shape, BF16),
            notes_shape,
            shape(cache_values.shape, BF16),
        ],
        [VMEM, HBM, HBM, HBM, HBM, HBM],
        [VMEM] * 5,
        [
            pltpu.VMEM((model, width), BF16),
            pltpu.VMEM((width // LANES, LANES), F32),
            pltpu.SMEM(block_count.shape, jnp.int32),
            pltpu.SemaphoreType.DMA((5,)),
        ],
    )(x, w_query_unit, output_weight, score_row, block_count, value_cache)
    bases = swap([base] * parts, "mp")
    mixtures = call(
        functools.partial(attend_kernel, owners),
        [slot] * owners,
        [VMEM] * (3 + owners),
        [VMEM] * owners,
    )(time_bias, history_key_cache, values, *slots[::-1])
    mixtures = swap(mixtures, "users", "helpers")
    product, sent = call(
        functools.partial(product_kernel, owners),
        [shape(sums, F32), shape(sums, BF16)],
        [VMEM] * (3 + owners),
        [VMEM] * 2,
    )(notes, gate, out_w, *mixtures[::-1])
    products = [product] + swap([sent] * parts, "mp")[1:]
    return call(
        functools.partial(score_kernel, parts),
        shape((blocks, block_rows), F32),
        [VMEM] * (2 + 2 * parts),
        VMEM,
    )(counts, x, *bases, *products)


def solution(mesh):
    return jax.shard_map(
        local,
        mesh=mesh,
        in_specs=(
            P(("groups", "users", "helpers"), None, None),
            P(("groups", "users", "helpers")),
            P(("groups", "users", "helpers")),
            P("groups"),
            P(("groups", "users"), None, "mp"),
            P(("groups", "users"), None, "mp"),
            P(None, None, "mp"),
            P("mp", None),
            P("mp", None),
            P("mp"),
        ),
        out_specs=P(("groups", "users", "helpers"), None),
        check_vma=False,
    )
```

```python
import functools

import jax
import jax.numpy as jnp
from jax import lax
from jax.experimental import pallas as pl
from jax.experimental.pallas import tpu as pltpu
from jax.sharding import PartitionSpec as P

EPSILON = 1e-05
MOST = 32
LANES = 128
TAIL = 16
CHUNKS = 4
F32 = jnp.float32
BF16 = jnp.bfloat16
VMEM = pl.BlockSpec(memory_space=pltpu.VMEM)
HBM = pl.BlockSpec(memory_space=pltpu.HBM)


def silu(v):
    return v / (1.0 + jnp.exp(-v))


def split3(v):
    high = v.astype(BF16).astype(F32)
    rest = v - high
    middle = rest.astype(BF16).astype(F32)
    return high, middle, rest - middle


def at_lane(shift):
    row = lax.broadcasted_iota(jnp.int32, (MOST, LANES), 0)
    return row + shift == lax.broadcasted_iota(jnp.int32, (MOST, LANES), 1)


def to_line(column, mask):
    return jnp.sum(jnp.where(mask, column, 0.0), axis=0, keepdims=True)


def to_column(line, mask):
    return jnp.sum(jnp.where(mask, line, 0.0), axis=1, keepdims=True)


def whole_tiles(rows):
    return -(-rows // TAIL) * TAIL


def query_kernel(owners, users_here, heads, user_source, map_source, candidates, weights, *rest):
    slots, (x, notes) = rest[:owners], rest[owners : owners + 2]
    w, block_user, own_map, x_sems, w_sems, sems = rest[owners + 2 :]
    blocks = candidates.shape[0]
    model, width = w.shape
    size = width // heads
    part = model // CHUNKS
    small = [
        pltpu.make_async_copy(user_source, block_user, sems.at[0]),
        pltpu.make_async_copy(map_source, own_map, sems.at[1]),
    ]
    x_copies = [
        pltpu.make_async_copy(
            candidates.at[b, pl.ds(0, MOST)], x.at[pl.ds(b * MOST, MOST)], x_sems.at[b]
        )
        for b in range(blocks)
    ]
    w_copies = [
        pltpu.make_async_copy(
            weights.at[0, pl.ds(i * part, part)], w.at[pl.ds(i * part, part)], w_sems.at[i]
        )
        for i in range(CHUNKS)
    ]
    for copy in small + x_copies + w_copies:
        copy.start()
    for copy in small:
        copy.wait()
    me = lax.axis_index("users")
    homes = []
    for b in range(blocks):
        storage = own_map[block_user[b]]
        homes.append(((storage // users_here) ^ me, storage % users_here))
        notes[b : b + 1, :] = jnp.full((1, LANES), homes[b][0], jnp.int32)
    for copy in x_copies:
        copy.wait()
    query = jnp.zeros((blocks * MOST, width), F32)
    for i, copy in enumerate(w_copies):
        copy.wait()
        cut = slice(i * part, (i + 1) * part)
        query += jnp.dot(x[:, cut], w[cut, :], preferred_element_type=F32)
    query = silu(query).astype(BF16)
    for s in range(owners):
        tag = jnp.zeros((TAIL, size), F32)
        for b, (slot, row) in enumerate(homes):
            tag = jnp.where(slot == s, row.astype(F32), tag)
        for h in range(heads):
            piece = jnp.zeros((MOST, size), BF16)
            for b, (slot, row) in enumerate(homes):
                mine = query[b * MOST : (b + 1) * MOST, h * size : (h + 1) * size]
                piece = jnp.where(slot == s, mine, piece)
            slots[s][h * MOST : (h + 1) * MOST, :] = piece
        slots[s][heads * MOST :, :] = tag.astype(BF16)


def attend_kernel(count, bias, keys, values, *rest):
    slots, outs = rest[:count], rest[count:]
    users_here, history, width = keys.shape
    heads = bias.shape[0]
    size = width // heads
    scale = size ** (-0.5)
    rows, weights = [], []
    for s in range(count):
        tag = jnp.max(slots[s][heads * MOST :, :].astype(F32))
        row = jnp.clip(tag.astype(jnp.int32), 0, users_here - 1)
        rows.append(row)
    none = jnp.zeros((MOST, size), BF16)
    for s in range(count):
        for h in range(0, heads, 2):
            one = slots[s][h * MOST : (h + 1) * MOST, :]
            two = slots[s][(h + 1) * MOST : (h + 2) * MOST, :]
            query = jnp.concatenate(
                [jnp.concatenate([one, none], axis=1), jnp.concatenate([none, two], axis=1)], axis=0
            )
            logits = lax.dot_general(
                query,
                keys[rows[s], :, h * size : (h + 2) * size],
                (((1,), (1,)), ((), ())),
                preferred_element_type=F32,
            )
            pair = jnp.concatenate(
                [jnp.broadcast_to(bias[h + i : h + i + 1, :], (MOST, history)) for i in range(2)]
            )
            weights.append(silu(logits * scale + pair).astype(BF16))
    mask = at_lane(0)
    for s in range(count):
        parts = []
        for h in range(0, heads, 2):
            mixed = jnp.dot(
                weights[(s * heads + h) // 2],
                values[rows[s], :, h * size : (h + 2) * size],
                preferred_element_type=F32,
            )
            parts += [mixed[:MOST, :size], mixed[MOST:, size:]]
        mean = jnp.sum(sum(parts), axis=1, keepdims=True) / width
        mean = mean.astype(BF16).astype(F32)
        for h, part in enumerate(parts):
            outs[s][h * MOST : (h + 1) * MOST, :] = (part - mean).astype(BF16)
        outs[s][heads * MOST :, :] = jnp.broadcast_to(to_line(mean, mask), (TAIL, size)).astype(BF16)


def gate_kernel(x, weights, out_source, score_source, count_source, value_source, *rest):
    gate_out, base_out, out_w, counts, values, w, vector, block_count, sems = rest
    rows = x.shape[0]
    width = w.shape[1]
    model = out_w.shape[1]
    copies = [
        pltpu.make_async_copy(count_source, block_count, sems.at[3]),
        pltpu.make_async_copy(score_source, vector, sems.at[2]),
        pltpu.make_async_copy(weights.at[1], w, sems.at[0]),
        pltpu.make_async_copy(out_source, out_w, sems.at[1]),
        pltpu.make_async_copy(value_source, values, sems.at[4]),
    ]
    for copy in copies:
        copy.start()
    copies[0].wait()
    for b in range(block_count.shape[0]):
        counts[b : b + 1, :] = jnp.full((1, LANES), block_count[b], jnp.int32)
    copies[1].wait()
    chunks = model // LANES
    pieces = jnp.concatenate(split3(vector[...]), axis=0).astype(BF16)
    base_out[chunks * rows :, :] = jnp.zeros((base_out.shape[0] - chunks * rows, LANES), BF16)
    base_out[chunks * rows : chunks * rows + pieces.shape[0], :] = pieces
    copies[2].wait()
    gate = silu(jnp.dot(x[...], w[...], preferred_element_type=F32))
    gate_out[...] = gate
    copies[3].wait()
    base = jnp.dot(gate.astype(BF16), out_w[...], preferred_element_type=F32)
    for c in range(chunks):
        base_out[c * rows : (c + 1) * rows, :] = base[:, c * LANES : (c + 1) * LANES].astype(BF16)
    copies[4].wait()


def product_kernel(order, notes, gate, out_weight, *rest):
    owners = len(order)
    slots = {s: ref for s, ref in zip(order, rest)}
    full, sent = rest[owners:]
    rows, width = gate.shape
    chunks = out_weight.shape[1] // LANES
    blocks = rows // MOST
    size = slots[0].shape[1]
    heads = width // size
    group = LANES // MOST
    lines = [[jnp.zeros((1, LANES), F32)] * 6 for _ in range(-(-blocks // group))]
    gated = []
    for b in range(blocks):
        place = notes[b : b + 1, :size]
        picked = slots[0][...].astype(F32)
        for s in range(1, owners):
            picked = jnp.where(place == s, slots[s][...].astype(F32), picked)
        parts = [picked[h * MOST : (h + 1) * MOST] for h in range(heads)]
        extra = jnp.sum(sum(parts), axis=1, keepdims=True) / width
        mean = to_column(picked[heads * MOST : heads * MOST + 1], at_lane(0)) + extra
        parts = [part - extra for part in parts]
        square = jnp.sum(sum(part * part for part in parts), axis=1, keepdims=True)
        mask = at_lane(b % group * MOST)
        values = (*split3(to_line(mean, mask)), *split3(to_line(square, mask)))
        lines[b // group] = [one + two for one, two in zip(lines[b // group], values)]
        gated.append(
            jnp.concatenate(
                [
                    part * gate[b * MOST : (b + 1) * MOST, h * size : (h + 1) * size]
                    for h, part in enumerate(parts)
                ],
                axis=1,
            )
        )
    product = jnp.dot(
        jnp.concatenate(gated, axis=0).astype(BF16), out_weight[...], preferred_element_type=F32
    )
    tail = jnp.concatenate([line for part in lines for line in part], axis=0)
    for ref, kind in ((full, F32), (sent, BF16)):
        for c in range(chunks):
            ref[c * rows : (c + 1) * rows, :] = product[:, c * LANES : (c + 1) * LANES].astype(kind)
        ref[chunks * rows :, :] = jnp.zeros((ref.shape[0] - chunks * rows, LANES), kind)
        ref[chunks * rows : chunks * rows + tail.shape[0], :] = tail.astype(kind)


def score_kernel(parts, counts, x, *rest):
    bases, products, out = rest[:parts], rest[parts : 2 * parts], rest[2 * parts]
    blocks, block_rows = out.shape
    rows, model = x.shape
    chunks = model // LANES
    own = chunks // parts
    group = LANES // MOST
    means, squares = [], []
    for p in products:
        tail = p[chunks * rows :, :].astype(F32)
        mean, square = [], []
        for b in range(blocks):
            mask = at_lane(b % group * MOST)
            first = b // group * 6
            line = tail[first : first + 1] + tail[first + 1 : first + 2] + tail[first + 2 : first + 3]
            mean.append(to_column(line, mask))
            first += 3
            line = tail[first : first + 1] + tail[first + 1 : first + 2] + tail[first + 2 : first + 3]
            square.append(to_column(line, mask))
        means.append(jnp.concatenate(mean, axis=0))
        squares.append(jnp.concatenate(square, axis=0))
    mean = sum(means) / parts
    offsets = [m - mean for m in means]
    spread = sum(squares) / model + sum(d * d for d in offsets) / parts
    scale = lax.rsqrt(spread + EPSILON)
    me = lax.axis_index("mp")
    vectors = [base[chunks * rows : chunks * rows + 3 * own, :].astype(F32) for base in bases]
    vectors = [v[:own] + v[own : 2 * own] + v[2 * own :] for v in vectors]
    score = jnp.zeros((rows, LANES), F32)
    for c in range(chunks):
        cut = slice(c * rows, (c + 1) * rows)
        total = sum(p[cut, :].astype(F32) for p in products)
        for d, base in zip(offsets, bases):
            total = total + d * base[cut, :].astype(F32)
        vector = vectors[0][c % own : c % own + 1]
        for s in range(1, parts):
            vector = jnp.where((me ^ s) == c // own, vectors[s][c % own : c % own + 1], vector)
        feature = x[:, c * LANES : (c + 1) * LANES].astype(F32)
        score = score + silu(feature + total * scale) * vector
    score = jnp.sum(score, axis=1, keepdims=True)
    mask = at_lane(0)
    lane = lax.broadcasted_iota(jnp.int32, (1, LANES), 1)
    for b in range(blocks):
        line = to_line(score[b * MOST : (b + 1) * MOST], mask)
        line = jnp.where(lane < counts[b : b + 1, :], line, 0.0)
        out[b : b + 1, :LANES] = line
        if block_rows > LANES:
            out[b : b + 1, LANES:] = jnp.zeros((1, block_rows - LANES), F32)


def swap(arrays, axis, cross=None):
    size = lax.axis_size(axis)
    out = [None] * size
    out[0] = arrays[0]
    for s in range(size - 1, 0, -1):
        if cross is None:
            out[s] = lax.ppermute(arrays[s], axis, [(k, k ^ s) for k in range(size)])
        else:
            cores = lax.axis_size(cross)
            pairs = [
                (k * cores + c, (k ^ s) * cores + cores - 1 - c)
                for k in range(size)
                for c in range(cores)
            ]
            out[s] = lax.ppermute(arrays[s], (axis, cross), pairs)
    return out


def local(
    candidates,
    block_user,
    block_count,
    own_map,
    history_key_cache,
    cache_values,
    w_query_unit,
    time_bias,
    output_weight,
    w_score,
):
    owners = lax.axis_size("users")
    parts = lax.axis_size("mp")
    blocks, block_rows, model = candidates.shape
    users_here, _, width = history_key_cache.shape
    rows = blocks * MOST
    shape = jax.ShapeDtypeStruct

    def call(kernel, out_shape, in_specs, out_specs, scratch=()):
        return pl.pallas_call(
            kernel,
            out_shape=out_shape,
            in_specs=in_specs,
            out_specs=out_specs,
            scratch_shapes=list(scratch),
            compiler_params=pltpu.CompilerParams(vmem_limit_bytes=8 * 1024 * 1024),
        )

    block_user, own_map, block_count, candidates, w_query_unit, output_weight, score_row, value_cache = (
        pltpu.with_memory_space_constraint(a, pltpu.HBM)
        for a in (
            block_user, own_map, block_count, candidates, w_query_unit, output_weight, w_score.reshape(width // LANES, LANES), cache_values,
        )
    )
    heads = time_bias.shape[0]
    chunks = model // LANES
    sums = (chunks * rows + whole_tiles(6 * -(-rows // LANES)), LANES)
    slot = shape((heads * MOST + TAIL, width // heads), BF16)
    notes_shape = shape((blocks, LANES), jnp.int32)
    *slots, x, notes = call(
        functools.partial(query_kernel, owners, users_here, heads),
        [slot] * owners + [shape((rows, model), BF16), notes_shape],
        [HBM] * 4,
        [VMEM] * (owners + 2),
        [
            pltpu.VMEM((model, width), BF16),
            pltpu.SMEM(block_user.shape, jnp.int32),
            pltpu.SMEM(own_map.shape, jnp.int32),
            pltpu.SemaphoreType.DMA((blocks,)),
            pltpu.SemaphoreType.DMA((CHUNKS,)),
            pltpu.SemaphoreType.DMA((2,)),
        ],
    )(block_user, own_map, candidates, w_query_unit)
    slots = swap(slots, "users", "helpers")
    gate, base, out_w, counts, values = call(
        gate_kernel,
        [
            shape((rows, width), F32),
            shape((chunks * rows + whole_tiles(3 * width // LANES), LANES), BF16),
            shape(output_weight.shape, BF16),
            notes_shape,
            shape(cache_values.shape, BF16),
        ],
        [VMEM, HBM, HBM, HBM, HBM, HBM],
        [VMEM] * 5,
        [
            pltpu.VMEM((model, width), BF16),
            pltpu.VMEM((width // LANES, LANES), F32),
            pltpu.SMEM(block_count.shape, jnp.int32),
            pltpu.SemaphoreType.DMA((5,)),
        ],
    )(x, w_query_unit, output_weight, score_row, block_count, value_cache)
    bases = swap([base] * parts, "mp")
    def attend(order):
        return call(
            functools.partial(attend_kernel, len(order)),
            [slot] * len(order),
            [VMEM] * (3 + len(order)),
            [VMEM] * len(order),
        )(time_bias, history_key_cache, values, *[slots[s] for s in order])

    far_first = list(range(owners - 1, 0, -1))
    half_first = sorted(far_first, key=lambda s: s != owners // 2)
    mixtures = dict(zip([0], attend([0])))
    mixtures.update(zip(half_first, attend(half_first)))
    mixtures = swap(mixtures, "users", "helpers")
    order = [*far_first, 0]
    product, sent = call(
        functools.partial(product_kernel, order),
        [shape(sums, F32), shape(sums, BF16)],
        [VMEM] * (3 + owners),
        [VMEM] * 2,
    )(notes, gate, out_w, *[mixtures[s] for s in order])
    products = [product] + swap([sent] * parts, "mp")[1:]
    return call(
        functools.partial(score_kernel, parts),
        shape((blocks, block_rows), F32),
        [VMEM] * (2 + 2 * parts),
        VMEM,
    )(counts, x, *bases, *products)


def solution(mesh):
    return jax.shard_map(
        local,
        mesh=mesh,
        in_specs=(
            P(("groups", "users", "helpers"), None, None),
            P(("groups", "users", "helpers")),
            P(("groups", "users", "helpers")),
            P("groups"),
            P(("groups", "users"), None, "mp"),
            P(("groups", "users"), None, "mp"),
            P(None, None, "mp"),
            P("mp", None),
            P("mp", None),
            P("mp"),
        ),
        out_specs=P(("groups", "users", "helpers"), None),
        check_vma=False,
    )
```

```python
import functools

import jax
import jax.numpy as jnp
from jax import lax
from jax.experimental import pallas as pl
from jax.experimental.pallas import tpu as pltpu
from jax.sharding import PartitionSpec as P

EPSILON = 1e-05
MOST = 32
LANES = 128
TAIL = 16
CHUNKS = 4
F32 = jnp.float32
BF16 = jnp.bfloat16
VMEM = pl.BlockSpec(memory_space=pltpu.VMEM)
HBM = pl.BlockSpec(memory_space=pltpu.HBM)


def silu(v):
    return v / (1.0 + jnp.exp(-v))


def split3(v):
    high = v.astype(BF16).astype(F32)
    rest = v - high
    middle = rest.astype(BF16).astype(F32)
    return high, middle, rest - middle


def at_lane(shift):
    row = lax.broadcasted_iota(jnp.int32, (MOST, LANES), 0)
    return row + shift == lax.broadcasted_iota(jnp.int32, (MOST, LANES), 1)


def to_line(column, mask):
    return jnp.sum(jnp.where(mask, column, 0.0), axis=0, keepdims=True)


def to_column(line, mask):
    return jnp.sum(jnp.where(mask, line, 0.0), axis=1, keepdims=True)


def filled(pieces, rows):
    spare = rows - sum(piece.shape[0] for piece in pieces)
    none = [jnp.zeros((spare, LANES), F32)] if spare > 0 else []
    return jnp.concatenate([*pieces, *none], axis=0)


def whole_tiles(rows):
    return -(-rows // TAIL) * TAIL


def query_kernel(owners, users_here, heads, user_source, map_source, candidates, weights, *rest):
    slots, (x, notes) = rest[:owners], rest[owners : owners + 2]
    w, block_user, own_map, x_sems, w_sems, sems = rest[owners + 2 :]
    blocks = candidates.shape[0]
    model, width = w.shape
    size = width // heads
    part = model // CHUNKS
    small = [
        pltpu.make_async_copy(user_source, block_user, sems.at[0]),
        pltpu.make_async_copy(map_source, own_map, sems.at[1]),
    ]
    x_copies = [
        pltpu.make_async_copy(
            candidates.at[b, pl.ds(0, MOST)], x.at[pl.ds(b * MOST, MOST)], x_sems.at[b]
        )
        for b in range(blocks)
    ]
    w_copies = [
        pltpu.make_async_copy(
            weights.at[0, pl.ds(i * part, part)], w.at[pl.ds(i * part, part)], w_sems.at[i]
        )
        for i in range(CHUNKS)
    ]
    for copy in small + x_copies + w_copies:
        copy.start()
    for copy in small:
        copy.wait()
    me = lax.axis_index("users")
    homes = []
    for b in range(blocks):
        storage = own_map[block_user[b]]
        homes.append(((storage // users_here) ^ me, storage % users_here))
        notes[b : b + 1, :] = jnp.full((1, LANES), homes[b][0], jnp.int32)
    for copy in x_copies:
        copy.wait()
    query = jnp.zeros((blocks * MOST, width), F32)
    for i, copy in enumerate(w_copies):
        copy.wait()
        cut = slice(i * part, (i + 1) * part)
        query += jnp.dot(x[:, cut], w[cut, :], preferred_element_type=F32)
    query = silu(query).astype(BF16)
    for s in range(owners):
        tag = jnp.zeros((TAIL, size), F32)
        for b, (slot, row) in enumerate(homes):
            tag = jnp.where(slot == s, row.astype(F32), tag)
        for h in range(heads):
            piece = jnp.zeros((MOST, size), BF16)
            for b, (slot, row) in enumerate(homes):
                mine = query[b * MOST : (b + 1) * MOST, h * size : (h + 1) * size]
                piece = jnp.where(slot == s, mine, piece)
            slots[s][h * MOST : (h + 1) * MOST, :] = piece
        slots[s][heads * MOST :, :] = tag.astype(BF16)


def attend_kernel(count, bias, keys, values, *rest):
    slots, outs = rest[:count], rest[count:]
    users_here, history, width = keys.shape
    heads = bias.shape[0]
    size = width // heads
    scale = size ** (-0.5)
    rows, weights = [], []
    for s in range(count):
        tag = jnp.max(slots[s][heads * MOST :, :].astype(F32))
        row = jnp.clip(tag.astype(jnp.int32), 0, users_here - 1)
        rows.append(row)
    none = jnp.zeros((MOST, size), BF16)
    for s in range(count):
        for h in range(0, heads, 2):
            one = slots[s][h * MOST : (h + 1) * MOST, :]
            two = slots[s][(h + 1) * MOST : (h + 2) * MOST, :]
            query = jnp.concatenate(
                [jnp.concatenate([one, none], axis=1), jnp.concatenate([none, two], axis=1)], axis=0
            )
            logits = lax.dot_general(
                query,
                keys[rows[s], :, h * size : (h + 2) * size],
                (((1,), (1,)), ((), ())),
                preferred_element_type=F32,
            )
            pair = jnp.concatenate(
                [jnp.broadcast_to(bias[h + i : h + i + 1, :], (MOST, history)) for i in range(2)]
            )
            weights.append(silu(logits * scale + pair).astype(BF16))
    mask = at_lane(0)
    for s in range(count):
        parts = []
        for h in range(0, heads, 2):
            mixed = jnp.dot(
                weights[(s * heads + h) // 2],
                values[rows[s], :, h * size : (h + 2) * size],
                preferred_element_type=F32,
            )
            parts += [mixed[:MOST, :size], mixed[MOST:, size:]]
        mean = jnp.sum(sum(parts), axis=1, keepdims=True) / width
        mean = mean.astype(BF16).astype(F32)
        for h, part in enumerate(parts):
            outs[s][h * MOST : (h + 1) * MOST, :] = (part - mean).astype(BF16)
        outs[s][heads * MOST :, :] = jnp.broadcast_to(to_line(mean, mask), (TAIL, size)).astype(BF16)


def gate_kernel(x, weights, out_source, score_source, count_source, value_source, *rest):
    gate_out, base_out, out_w, counts, values, w, vector, block_count, sems = rest
    rows = x.shape[0]
    width = w.shape[1]
    model = out_w.shape[1]
    copies = [
        pltpu.make_async_copy(count_source, block_count, sems.at[3]),
        pltpu.make_async_copy(score_source, vector, sems.at[2]),
        pltpu.make_async_copy(weights.at[1], w, sems.at[0]),
        pltpu.make_async_copy(out_source, out_w, sems.at[1]),
        pltpu.make_async_copy(value_source, values, sems.at[4]),
    ]
    for copy in copies:
        copy.start()
    copies[0].wait()
    for b in range(block_count.shape[0]):
        counts[b : b + 1, :] = jnp.full((1, LANES), block_count[b], jnp.int32)
    copies[1].wait()
    chunks = model // LANES
    pieces = filled(split3(vector[...]), base_out.shape[0] - chunks * rows)
    base_out[chunks * rows :, :] = pieces.astype(BF16)
    copies[2].wait()
    gate = silu(jnp.dot(x[...], w[...], preferred_element_type=F32))
    gate_out[...] = gate
    copies[3].wait()
    base = jnp.dot(gate.astype(BF16), out_w[...], preferred_element_type=F32)
    for c in range(chunks):
        base_out[c * rows : (c + 1) * rows, :] = base[:, c * LANES : (c + 1) * LANES].astype(BF16)
    copies[4].wait()


def product_kernel(order, notes, gate, out_weight, *rest):
    owners = len(order)
    slots = {s: ref for s, ref in zip(order, rest)}
    full, sent = rest[owners:]
    rows, width = gate.shape
    chunks = out_weight.shape[1] // LANES
    blocks = rows // MOST
    size = slots[0].shape[1]
    heads = width // size
    group = LANES // MOST
    lines = [[jnp.zeros((1, LANES), F32)] * 6 for _ in range(-(-blocks // group))]
    gated = []
    for b in range(blocks):
        place = notes[b : b + 1, :size]
        picked = slots[0][...].astype(F32)
        for s in range(1, owners):
            picked = jnp.where(place == s, slots[s][...].astype(F32), picked)
        parts = [picked[h * MOST : (h + 1) * MOST] for h in range(heads)]
        extra = jnp.sum(sum(parts), axis=1, keepdims=True) / width
        mean = to_column(picked[heads * MOST : heads * MOST + 1], at_lane(0)) + extra
        parts = [part - extra for part in parts]
        square = jnp.sum(sum(part * part for part in parts), axis=1, keepdims=True)
        mask = at_lane(b % group * MOST)
        values = (*split3(to_line(mean, mask)), *split3(to_line(square, mask)))
        lines[b // group] = [one + two for one, two in zip(lines[b // group], values)]
        gated.append(
            jnp.concatenate(
                [
                    part * gate[b * MOST : (b + 1) * MOST, h * size : (h + 1) * size]
                    for h, part in enumerate(parts)
                ],
                axis=1,
            )
        )
    product = jnp.dot(
        jnp.concatenate(gated, axis=0).astype(BF16), out_weight[...], preferred_element_type=F32
    )
    tail = filled([line for part in lines for line in part], sent.shape[0] - chunks * rows)
    for ref, kind in ((full, F32), (sent, BF16)):
        for c in range(chunks):
            ref[c * rows : (c + 1) * rows, :] = product[:, c * LANES : (c + 1) * LANES].astype(kind)
        ref[chunks * rows :, :] = tail.astype(kind)


def score_kernel(parts, counts, x, *rest):
    bases, products, out = rest[:parts], rest[parts : 2 * parts], rest[2 * parts]
    blocks, block_rows = out.shape
    rows, model = x.shape
    chunks = model // LANES
    own = chunks // parts
    group = LANES // MOST
    means, squares = [], []
    for p in products:
        tail = p[chunks * rows :, :].astype(F32)
        mean, square = [], []
        for b in range(blocks):
            mask = at_lane(b % group * MOST)
            first = b // group * 6
            line = tail[first : first + 1] + tail[first + 1 : first + 2] + tail[first + 2 : first + 3]
            mean.append(to_column(line, mask))
            first += 3
            line = tail[first : first + 1] + tail[first + 1 : first + 2] + tail[first + 2 : first + 3]
            square.append(to_column(line, mask))
        means.append(jnp.concatenate(mean, axis=0))
        squares.append(jnp.concatenate(square, axis=0))
    mean = sum(means) / parts
    offsets = [m - mean for m in means]
    spread = sum(squares) / model + sum(d * d for d in offsets) / parts
    scale = lax.rsqrt(spread + EPSILON)
    me = lax.axis_index("mp")
    vectors = [base[chunks * rows :, :].astype(F32) for base in bases]
    vectors = [v[:own] + v[own : 2 * own] + v[2 * own : 3 * own] for v in vectors]
    score = jnp.zeros((rows, LANES), F32)
    for c in range(chunks):
        cut = slice(c * rows, (c + 1) * rows)
        total = sum(p[cut, :].astype(F32) for p in products)
        for d, base in zip(offsets, bases):
            total = total + d * base[cut, :].astype(F32)
        vector = vectors[0][c % own : c % own + 1]
        for s in range(1, parts):
            vector = jnp.where((me ^ s) == c // own, vectors[s][c % own : c % own + 1], vector)
        feature = x[:, c * LANES : (c + 1) * LANES].astype(F32)
        score = score + silu(feature + total * scale) * vector
    score = jnp.sum(score, axis=1, keepdims=True)
    mask = at_lane(0)
    lane = lax.broadcasted_iota(jnp.int32, (1, LANES), 1)
    for b in range(blocks):
        line = to_line(score[b * MOST : (b + 1) * MOST], mask)
        line = jnp.where(lane < counts[b : b + 1, :], line, 0.0)
        out[b : b + 1, :LANES] = line
        if block_rows > LANES:
            out[b : b + 1, LANES:] = jnp.zeros((1, block_rows - LANES), F32)


def swap(arrays, axis, cross=None):
    size = lax.axis_size(axis)
    out = [None] * size
    out[0] = arrays[0]
    for s in range(size - 1, 0, -1):
        if cross is None:
            out[s] = lax.ppermute(arrays[s], axis, [(k, k ^ s) for k in range(size)])
        else:
            cores = lax.axis_size(cross)
            pairs = [
                (k * cores + c, (k ^ s) * cores + cores - 1 - c)
                for k in range(size)
                for c in range(cores)
            ]
            out[s] = lax.ppermute(arrays[s], (axis, cross), pairs)
    return out


def local(
    candidates,
    block_user,
    block_count,
    own_map,
    history_key_cache,
    cache_values,
    w_query_unit,
    time_bias,
    output_weight,
    w_score,
):
    owners = lax.axis_size("users")
    parts = lax.axis_size("mp")
    blocks, block_rows, model = candidates.shape
    users_here, _, width = history_key_cache.shape
    rows = blocks * MOST
    shape = jax.ShapeDtypeStruct

    def call(kernel, out_shape, in_specs, out_specs, scratch=()):
        return pl.pallas_call(
            kernel,
            out_shape=out_shape,
            in_specs=in_specs,
            out_specs=out_specs,
            scratch_shapes=list(scratch),
            compiler_params=pltpu.CompilerParams(vmem_limit_bytes=8 * 1024 * 1024),
        )

    def fetched(array):
        return pltpu.with_memory_space_constraint(array, pltpu.HBM)

    block_user, own_map, block_count = fetched(block_user), fetched(own_map), fetched(block_count)
    candidates, w_query_unit = fetched(candidates), fetched(w_query_unit)
    output_weight, value_cache = fetched(output_weight), fetched(cache_values)
    score_row = fetched(w_score.reshape(width // LANES, LANES))
    heads = time_bias.shape[0]
    chunks = model // LANES
    sums = (chunks * rows + whole_tiles(6 * -(-rows // LANES)), LANES)
    slot = shape((heads * MOST + TAIL, width // heads), BF16)
    notes_shape = shape((blocks, LANES), jnp.int32)
    *slots, x, notes = call(
        functools.partial(query_kernel, owners, users_here, heads),
        [slot] * owners + [shape((rows, model), BF16), notes_shape],
        [HBM] * 4,
        [VMEM] * (owners + 2),
        [
            pltpu.VMEM((model, width), BF16),
            pltpu.SMEM(block_user.shape, jnp.int32),
            pltpu.SMEM(own_map.shape, jnp.int32),
            pltpu.SemaphoreType.DMA((blocks,)),
            pltpu.SemaphoreType.DMA((CHUNKS,)),
            pltpu.SemaphoreType.DMA((2,)),
        ],
    )(block_user, own_map, candidates, w_query_unit)
    slots = swap(slots, "users", "helpers")
    gate, base, out_w, counts, values = call(
        gate_kernel,
        [
            shape((rows, width), F32),
            shape((chunks * rows + whole_tiles(3 * width // LANES), LANES), BF16),
            shape(output_weight.shape, BF16),
            notes_shape,
            shape(cache_values.shape, BF16),
        ],
        [VMEM, HBM, HBM, HBM, HBM, HBM],
        [VMEM] * 5,
        [
            pltpu.VMEM((model, width), BF16),
            pltpu.VMEM((width // LANES, LANES), F32),
            pltpu.SMEM(block_count.shape, jnp.int32),
            pltpu.SemaphoreType.DMA((5,)),
        ],
    )(x, w_query_unit, output_weight, score_row, block_count, value_cache)
    bases = swap([base] * parts, "mp")

    def attend(order):
        return call(
            functools.partial(attend_kernel, len(order)),
            [slot] * len(order),
            [VMEM] * (3 + len(order)),
            [VMEM] * len(order),
        )(time_bias, history_key_cache, values, *[slots[s] for s in order])

    far_first = list(range(owners - 1, 0, -1))
    half_first = sorted(far_first, key=lambda s: s != owners // 2)
    mixtures = dict(zip([0], attend([0])))
    mixtures.update(zip(half_first, attend(half_first)))
    mixtures = swap(mixtures, "users", "helpers")
    order = [*far_first, 0]
    product, sent = call(
        functools.partial(product_kernel, order),
        [shape(sums, F32), shape(sums, BF16)],
        [VMEM] * (3 + owners),
        [VMEM] * 2,
    )(notes, gate, out_w, *[mixtures[s] for s in order])
    products = [product] + swap([sent] * parts, "mp")[1:]
    return call(
        functools.partial(score_kernel, parts),
        shape((blocks, block_rows), F32),
        [VMEM] * (2 + 2 * parts),
        VMEM,
    )(counts, x, *bases, *products)


def solution(mesh):
    return jax.shard_map(
        local,
        mesh=mesh,
        in_specs=(
            P(("groups", "users", "helpers"), None, None),
            P(("groups", "users", "helpers")),
            P(("groups", "users", "helpers")),
            P("groups"),
            P(("groups", "users"), None, "mp"),
            P(("groups", "users"), None, "mp"),
            P(None, None, "mp"),
            P("mp", None),
            P("mp", None),
            P("mp"),
        ),
        out_specs=P(("groups", "users", "helpers"), None),
        check_vma=False,
    )
```

```python
import functools

import jax
import jax.numpy as jnp
from jax import lax
from jax.experimental import pallas as pl
from jax.experimental.pallas import tpu as pltpu
from jax.sharding import PartitionSpec as P

EPSILON = 1e-05
MOST = 32
LANES = 128
TAIL = 16
CHUNKS = 4
F32 = jnp.float32
BF16 = jnp.bfloat16
VMEM = pl.BlockSpec(memory_space=pltpu.VMEM)
HBM = pl.BlockSpec(memory_space=pltpu.HBM)


def silu(v):
    return v / (1.0 + jnp.exp(-v))


def split3(v):
    high = v.astype(BF16).astype(F32)
    rest = v - high
    middle = rest.astype(BF16).astype(F32)
    return high, middle, rest - middle


def at_lane(shift):
    row = lax.broadcasted_iota(jnp.int32, (MOST, LANES), 0)
    return row + shift == lax.broadcasted_iota(jnp.int32, (MOST, LANES), 1)


def to_line(column, mask):
    return jnp.sum(jnp.where(mask, column, 0.0), axis=0, keepdims=True)


def to_column(line, mask):
    return jnp.sum(jnp.where(mask, line, 0.0), axis=1, keepdims=True)


def filled(pieces, rows):
    spare = rows - sum(piece.shape[0] for piece in pieces)
    none = [jnp.zeros((spare, LANES), F32)] if spare > 0 else []
    return jnp.concatenate([*pieces, *none], axis=0)


def whole_tiles(rows):
    return -(-rows // TAIL) * TAIL


def query_kernel(owners, users_here, heads, user_source, map_source, candidates, weights, *rest):
    slots, (x, notes) = rest[:owners], rest[owners : owners + 2]
    w, block_user, own_map, x_sems, w_sems, sems = rest[owners + 2 :]
    blocks = candidates.shape[0]
    model, width = w.shape
    size = width // heads
    part = model // CHUNKS
    small = [
        pltpu.make_async_copy(user_source, block_user, sems.at[0]),
        pltpu.make_async_copy(map_source, own_map, sems.at[1]),
    ]
    x_copies = [
        pltpu.make_async_copy(
            candidates.at[b, pl.ds(0, MOST)], x.at[pl.ds(b * MOST, MOST)], x_sems.at[b]
        )
        for b in range(blocks)
    ]
    w_copies = [
        pltpu.make_async_copy(
            weights.at[0, pl.ds(i * part, part)], w.at[pl.ds(i * part, part)], w_sems.at[i]
        )
        for i in range(CHUNKS)
    ]
    for copy in small + x_copies + w_copies:
        copy.start()
    for copy in small:
        copy.wait()
    me = lax.axis_index("users")
    homes = []
    for b in range(blocks):
        storage = own_map[block_user[b]]
        homes.append(((storage // users_here) ^ me, storage % users_here))
        notes[b : b + 1, :] = jnp.full((1, LANES), homes[b][0], jnp.int32)
    for copy in x_copies:
        copy.wait()
    query = jnp.zeros((blocks * MOST, width), F32)
    for i, copy in enumerate(w_copies):
        copy.wait()
        cut = slice(i * part, (i + 1) * part)
        query += jnp.dot(x[:, cut], w[cut, :], preferred_element_type=F32)
    query = silu(query).astype(BF16)
    for s in range(owners):
        tag = jnp.zeros((TAIL, size), F32)
        for b, (slot, row) in enumerate(homes):
            tag = jnp.where(slot == s, row.astype(F32), tag)
        for h in range(heads):
            piece = jnp.zeros((MOST, size), BF16)
            for b, (slot, row) in enumerate(homes):
                mine = query[b * MOST : (b + 1) * MOST, h * size : (h + 1) * size]
                piece = jnp.where(slot == s, mine, piece)
            slots[s][h * MOST : (h + 1) * MOST, :] = piece
        slots[s][heads * MOST :, :] = tag.astype(BF16)


def attend_kernel(count, bias, keys, values, *rest):
    slots, outs = rest[:count], rest[count:]
    users_here, history, width = keys.shape
    heads = bias.shape[0]
    size = width // heads
    scale = size ** (-0.5)
    rows, weights = [], []
    for s in range(count):
        tag = jnp.max(slots[s][heads * MOST :, :].astype(F32))
        row = jnp.clip(tag.astype(jnp.int32), 0, users_here - 1)
        rows.append(row)
    none = jnp.zeros((MOST, size), BF16)
    for s in range(count):
        for h in range(0, heads, 2):
            one = slots[s][h * MOST : (h + 1) * MOST, :]
            two = slots[s][(h + 1) * MOST : (h + 2) * MOST, :]
            query = jnp.concatenate(
                [jnp.concatenate([one, none], axis=1), jnp.concatenate([none, two], axis=1)], axis=0
            )
            logits = lax.dot_general(
                query,
                keys[rows[s], :, h * size : (h + 2) * size],
                (((1,), (1,)), ((), ())),
                preferred_element_type=F32,
            )
            pair = jnp.concatenate(
                [jnp.broadcast_to(bias[h + i : h + i + 1, :], (MOST, history)) for i in range(2)]
            )
            weights.append(silu(logits * scale + pair).astype(BF16))
    mask = at_lane(0)
    for s in range(count):
        parts = []
        for h in range(0, heads, 2):
            mixed = jnp.dot(
                weights[(s * heads + h) // 2],
                values[rows[s], :, h * size : (h + 2) * size],
                preferred_element_type=F32,
            )
            parts += [mixed[:MOST, :size], mixed[MOST:, size:]]
        mean = jnp.sum(sum(parts), axis=1, keepdims=True) / width
        mean = mean.astype(BF16).astype(F32)
        for h, part in enumerate(parts):
            outs[s][h * MOST : (h + 1) * MOST, :] = (part - mean).astype(BF16)
        outs[s][heads * MOST :, :] = jnp.broadcast_to(to_line(mean, mask), (TAIL, size)).astype(BF16)


def gate_kernel(x, weights, out_source, score_source, count_source, value_source, *rest):
    gate_out, base_out, out_w, counts, values, w, vector, block_count, sems = rest
    rows = x.shape[0]
    width = w.shape[1]
    model = out_w.shape[1]
    copies = [
        pltpu.make_async_copy(count_source, block_count, sems.at[3]),
        pltpu.make_async_copy(score_source, vector, sems.at[2]),
        pltpu.make_async_copy(weights.at[1], w, sems.at[0]),
        pltpu.make_async_copy(out_source, out_w, sems.at[1]),
        pltpu.make_async_copy(value_source, values, sems.at[4]),
    ]
    for copy in copies:
        copy.start()
    copies[0].wait()
    for b in range(block_count.shape[0]):
        counts[b : b + 1, :] = jnp.full((1, LANES), block_count[b], jnp.int32)
    copies[1].wait()
    chunks = model // LANES
    pieces = filled(split3(vector[...]), base_out.shape[0] - chunks * rows)
    base_out[chunks * rows :, :] = pieces.astype(BF16)
    copies[2].wait()
    gate = silu(jnp.dot(x[...], w[...], preferred_element_type=F32))
    gate_out[...] = gate
    copies[3].wait()
    base = jnp.dot(gate.astype(BF16), out_w[...], preferred_element_type=F32)
    for c in range(chunks):
        base_out[c * rows : (c + 1) * rows, :] = base[:, c * LANES : (c + 1) * LANES].astype(BF16)
    copies[4].wait()


def product_kernel(order, notes, gate, out_weight, *rest):
    owners = len(order)
    slots = {s: ref for s, ref in zip(order, rest)}
    full, sent = rest[owners:]
    rows, width = gate.shape
    chunks = out_weight.shape[1] // LANES
    blocks = rows // MOST
    size = slots[0].shape[1]
    heads = width // size
    group = LANES // MOST
    lines = [[jnp.zeros((1, LANES), F32)] * 7 for _ in range(-(-blocks // group))]
    gated = []
    for b in range(blocks):
        place = notes[b : b + 1, :size]
        picked = slots[0][...].astype(F32)
        for s in range(1, owners):
            picked = jnp.where(place == s, slots[s][...].astype(F32), picked)
        parts = [picked[h * MOST : (h + 1) * MOST] for h in range(heads)]
        extra = jnp.sum(sum(parts), axis=1, keepdims=True)
        centre = to_column(picked[heads * MOST : heads * MOST + 1], at_lane(0))
        square = jnp.sum(sum(part * part for part in parts), axis=1, keepdims=True)
        mask = at_lane(b % group * MOST)
        values = (
            to_line(centre, mask),
            *split3(to_line(extra, mask)),
            *split3(to_line(square, mask)),
        )
        lines[b // group] = [one + two for one, two in zip(lines[b // group], values)]
        gated.append(
            jnp.concatenate(
                [
                    part * gate[b * MOST : (b + 1) * MOST, h * size : (h + 1) * size]
                    for h, part in enumerate(parts)
                ],
                axis=1,
            )
        )
    product = jnp.dot(
        jnp.concatenate(gated, axis=0).astype(BF16), out_weight[...], preferred_element_type=F32
    )
    tail = filled([line for part in lines for line in part], sent.shape[0] - chunks * rows)
    for ref, kind in ((full, F32), (sent, BF16)):
        for c in range(chunks):
            ref[c * rows : (c + 1) * rows, :] = product[:, c * LANES : (c + 1) * LANES].astype(kind)
        ref[chunks * rows :, :] = tail.astype(kind)


def score_kernel(parts, counts, x, *rest):
    bases, products, out = rest[:parts], rest[parts : 2 * parts], rest[2 * parts]
    blocks, block_rows = out.shape
    rows, model = x.shape
    chunks = model // LANES
    own = chunks // parts
    group = LANES // MOST
    masks = [at_lane(b % group * MOST) for b in range(blocks)]
    tails = [p[chunks * rows :, :].astype(F32) for p in products]
    shifts, scales = [[] for _ in products], []
    for first in range(0, blocks, group):
        top = first // group * 7
        lines = [[tail[top + i : top + i + 1] for i in range(7)] for tail in tails]
        centres = [line[0] for line in lines]
        extras = [line[1] + line[2] + line[3] for line in lines]
        squares = [line[4] + line[5] + line[6] for line in lines]
        mean = sum(c * (model // parts) + e for c, e in zip(centres, extras)) / model
        deltas = [c - mean for c in centres]
        spread = sum(
            q + d * (2.0 * e + d * (model // parts)) for q, e, d in zip(squares, extras, deltas)
        )
        scale = lax.rsqrt(spread / model + EPSILON)
        for b in range(first, min(first + group, blocks)):
            scales.append(to_column(scale, masks[b]))
            for shift, delta in zip(shifts, deltas):
                shift.append(to_column(delta, masks[b]))
    offsets = [jnp.concatenate(shift, axis=0) for shift in shifts]
    scale = jnp.concatenate(scales, axis=0)
    me = lax.axis_index("mp")
    vectors = [base[chunks * rows :, :].astype(F32) for base in bases]
    vectors = [v[:own] + v[own : 2 * own] + v[2 * own : 3 * own] for v in vectors]
    score = jnp.zeros((rows, LANES), F32)
    for c in range(chunks):
        cut = slice(c * rows, (c + 1) * rows)
        total = sum(p[cut, :].astype(F32) for p in products)
        for d, base in zip(offsets, bases):
            total = total + d * base[cut, :].astype(F32)
        vector = vectors[0][c % own : c % own + 1]
        for s in range(1, parts):
            vector = jnp.where((me ^ s) == c // own, vectors[s][c % own : c % own + 1], vector)
        feature = x[:, c * LANES : (c + 1) * LANES].astype(F32)
        score = score + silu(feature + total * scale) * vector
    score = jnp.sum(score, axis=1, keepdims=True)
    mask = at_lane(0)
    lane = lax.broadcasted_iota(jnp.int32, (1, LANES), 1)
    for b in range(blocks):
        line = to_line(score[b * MOST : (b + 1) * MOST], mask)
        line = jnp.where(lane < counts[b : b + 1, :], line, 0.0)
        out[b : b + 1, :LANES] = line
        if block_rows > LANES:
            out[b : b + 1, LANES:] = jnp.zeros((1, block_rows - LANES), F32)


def swap(arrays, axis):
    size = lax.axis_size(axis)
    return [arrays[0]] + [
        lax.ppermute(arrays[s], axis, [(k, k ^ s) for k in range(size)]) for s in range(1, size)
    ]


def local(
    candidates,
    block_user,
    block_count,
    own_map,
    history_key_cache,
    cache_values,
    w_query_unit,
    time_bias,
    output_weight,
    w_score,
):
    owners = lax.axis_size("users")
    parts = lax.axis_size("mp")
    blocks, block_rows, model = candidates.shape
    users_here, _, width = history_key_cache.shape
    rows = blocks * MOST
    shape = jax.ShapeDtypeStruct

    def call(kernel, out_shape, in_specs, out_specs, scratch=()):
        return pl.pallas_call(
            kernel,
            out_shape=out_shape,
            in_specs=in_specs,
            out_specs=out_specs,
            scratch_shapes=list(scratch),
            compiler_params=pltpu.CompilerParams(vmem_limit_bytes=8 * 1024 * 1024),
        )

    def fetched(array):
        return pltpu.with_memory_space_constraint(array, pltpu.HBM)

    block_user, own_map, block_count = fetched(block_user), fetched(own_map), fetched(block_count)
    candidates, w_query_unit = fetched(candidates), fetched(w_query_unit)
    output_weight, value_cache = fetched(output_weight), fetched(cache_values)
    score_row = fetched(w_score.reshape(width // LANES, LANES))
    heads = time_bias.shape[0]
    chunks = model // LANES
    sums = (chunks * rows + whole_tiles(7 * -(-rows // LANES)), LANES)
    slot = shape((heads * MOST + TAIL, width // heads), BF16)
    notes_shape = shape((blocks, LANES), jnp.int32)
    *slots, x, notes = call(
        functools.partial(query_kernel, owners, users_here, heads),
        [slot] * owners + [shape((rows, model), BF16), notes_shape],
        [HBM] * 4,
        [VMEM] * (owners + 2),
        [
            pltpu.VMEM((model, width), BF16),
            pltpu.SMEM(block_user.shape, jnp.int32),
            pltpu.SMEM(own_map.shape, jnp.int32),
            pltpu.SemaphoreType.DMA((blocks,)),
            pltpu.SemaphoreType.DMA((CHUNKS,)),
            pltpu.SemaphoreType.DMA((2,)),
        ],
    )(block_user, own_map, candidates, w_query_unit)
    slots = swap(slots, "users")
    gate, base, out_w, counts, values = call(
        gate_kernel,
        [
            shape((rows, width), F32),
            shape((chunks * rows + whole_tiles(3 * width // LANES), LANES), BF16),
            shape(output_weight.shape, BF16),
            notes_shape,
            shape(cache_values.shape, BF16),
        ],
        [VMEM, HBM, HBM, HBM, HBM, HBM],
        [VMEM] * 5,
        [
            pltpu.VMEM((model, width), BF16),
            pltpu.VMEM((width // LANES, LANES), F32),
            pltpu.SMEM(block_count.shape, jnp.int32),
            pltpu.SemaphoreType.DMA((5,)),
        ],
    )(x, w_query_unit, output_weight, score_row, block_count, value_cache)
    bases = swap([base] * parts, "mp")

    def attend(order):
        return call(
            functools.partial(attend_kernel, len(order)),
            [slot] * len(order),
            [VMEM] * (3 + len(order)),
            [VMEM] * len(order),
        )(time_bias, history_key_cache, values, *[slots[s] for s in order])

    far_first = list(range(owners - 1, 0, -1))
    half_first = sorted(far_first, key=lambda s: s != owners // 2)
    mixtures = dict(zip([0], attend([0])))
    mixtures.update(zip(half_first, attend(half_first)))
    mixtures = swap(mixtures, "users")
    order = [*far_first, 0]
    product, sent = call(
        functools.partial(product_kernel, order),
        [shape(sums, F32), shape(sums, BF16)],
        [VMEM] * (3 + owners),
        [VMEM] * 2,
    )(notes, gate, out_w, *[mixtures[s] for s in order])
    products = [product] + swap([sent] * parts, "mp")[1:]
    return call(
        functools.partial(score_kernel, parts),
        shape((blocks, block_rows), F32),
        [VMEM] * (2 + 2 * parts),
        VMEM,
    )(counts, x, *bases, *products)


def solution(mesh):
    return jax.shard_map(
        local,
        mesh=mesh,
        in_specs=(
            P(("groups", "users", "helpers"), None, None),
            P(("groups", "users", "helpers")),
            P(("groups", "users", "helpers")),
            P("groups"),
            P(("groups", "users"), None, "mp"),
            P(("groups", "users"), None, "mp"),
            P(None, None, "mp"),
            P("mp", None),
            P("mp", None),
            P("mp"),
        ),
        out_specs=P(("groups", "users", "helpers"), None),
        check_vma=False,
    )
```

```python
import functools

import jax
import jax.numpy as jnp
from jax import lax
from jax.experimental import pallas as pl
from jax.experimental.pallas import tpu as pltpu
from jax.sharding import PartitionSpec as P

EPSILON = 1e-05
MOST = 32
LANES = 128
TAIL = 16
CHUNKS = 4
F32 = jnp.float32
BF16 = jnp.bfloat16
VMEM = pl.BlockSpec(memory_space=pltpu.VMEM)
HBM = pl.BlockSpec(memory_space=pltpu.HBM)


def silu(v):
    return v / (1.0 + jnp.exp(-v))


def split3(v):
    high = v.astype(BF16).astype(F32)
    rest = v - high
    middle = rest.astype(BF16).astype(F32)
    return high, middle, rest - middle


def at_lane(shift):
    row = lax.broadcasted_iota(jnp.int32, (MOST, LANES), 0)
    return row + shift == lax.broadcasted_iota(jnp.int32, (MOST, LANES), 1)


def to_line(column, mask):
    return jnp.sum(jnp.where(mask, column, 0.0), axis=0, keepdims=True)


def to_column(line, mask):
    return jnp.sum(jnp.where(mask, line, 0.0), axis=1, keepdims=True)


def filled(pieces, rows):
    spare = rows - sum(piece.shape[0] for piece in pieces)
    none = [jnp.zeros((spare, LANES), F32)] if spare > 0 else []
    return jnp.concatenate([*pieces, *none], axis=0)


def whole_tiles(rows):
    return -(-rows // TAIL) * TAIL


def query_kernel(owners, users_here, heads, user_source, map_source, candidates, weights, *rest):
    slots, (x, notes) = rest[:owners], rest[owners : owners + 2]
    w, block_user, own_map, x_sems, w_sems, sems = rest[owners + 2 :]
    blocks = candidates.shape[0]
    model, width = w.shape
    size = width // heads
    part = model // CHUNKS
    small = [
        pltpu.make_async_copy(user_source, block_user, sems.at[0]),
        pltpu.make_async_copy(map_source, own_map, sems.at[1]),
    ]
    x_copies = [
        pltpu.make_async_copy(
            candidates.at[b, pl.ds(0, MOST)], x.at[pl.ds(b * MOST, MOST)], x_sems.at[b]
        )
        for b in range(blocks)
    ]
    w_copies = [
        pltpu.make_async_copy(
            weights.at[0, pl.ds(i * part, part)], w.at[pl.ds(i * part, part)], w_sems.at[i]
        )
        for i in range(CHUNKS)
    ]
    for copy in small + x_copies + w_copies:
        copy.start()
    for copy in small:
        copy.wait()
    me = lax.axis_index("users")
    homes = []
    for b in range(blocks):
        storage = own_map[block_user[b]]
        homes.append(((storage // users_here) ^ me, storage % users_here))
        notes[b : b + 1, :] = jnp.full((1, LANES), homes[b][0], jnp.int32)
    for copy in x_copies:
        copy.wait()
    query = jnp.zeros((blocks * MOST, width), F32)
    for i, copy in enumerate(w_copies):
        copy.wait()
        cut = slice(i * part, (i + 1) * part)
        query += jnp.dot(x[:, cut], w[cut, :], preferred_element_type=F32)
    query = silu(query).astype(BF16)
    for s in range(owners):
        tag = jnp.zeros((TAIL, size), F32)
        for b, (slot, row) in enumerate(homes):
            tag = jnp.where(slot == s, row.astype(F32), tag)
        for h in range(heads):
            piece = jnp.zeros((MOST, size), BF16)
            for b, (slot, row) in enumerate(homes):
                mine = query[b * MOST : (b + 1) * MOST, h * size : (h + 1) * size]
                piece = jnp.where(slot == s, mine, piece)
            slots[s][h * MOST : (h + 1) * MOST, :] = piece
        slots[s][heads * MOST :, :] = tag.astype(BF16)


def attend_kernel(count, bias, keys, values, *rest):
    slots, outs = rest[:count], rest[count:]
    users_here, history, width = keys.shape
    heads = bias.shape[0]
    size = width // heads
    scale = size ** (-0.5)
    rows, weights = [], []
    for s in range(count):
        tag = jnp.max(slots[s][heads * MOST :, :].astype(F32))
        row = jnp.clip(tag.astype(jnp.int32), 0, users_here - 1)
        rows.append(row)
    none = jnp.zeros((MOST, size), BF16)
    for s in range(count):
        for h in range(0, heads, 2):
            one = slots[s][h * MOST : (h + 1) * MOST, :]
            two = slots[s][(h + 1) * MOST : (h + 2) * MOST, :]
            query = jnp.concatenate(
                [jnp.concatenate([one, none], axis=1), jnp.concatenate([none, two], axis=1)], axis=0
            )
            logits = lax.dot_general(
                query,
                keys[rows[s], :, h * size : (h + 2) * size],
                (((1,), (1,)), ((), ())),
                preferred_element_type=F32,
            )
            pair = jnp.concatenate(
                [jnp.broadcast_to(bias[h + i : h + i + 1, :], (MOST, history)) for i in range(2)]
            )
            weights.append(silu(logits * scale + pair).astype(BF16))
    mask = at_lane(0)
    for s in range(count):
        parts = []
        for h in range(0, heads, 2):
            mixed = jnp.dot(
                weights[(s * heads + h) // 2],
                values[rows[s], :, h * size : (h + 2) * size],
                preferred_element_type=F32,
            )
            parts += [mixed[:MOST, :size], mixed[MOST:, size:]]
        mean = jnp.sum(sum(parts), axis=1, keepdims=True) / width
        mean = mean.astype(BF16).astype(F32)
        for h, part in enumerate(parts):
            outs[s][h * MOST : (h + 1) * MOST, :] = (part - mean).astype(BF16)
        outs[s][heads * MOST :, :] = jnp.broadcast_to(to_line(mean, mask), (TAIL, size)).astype(BF16)


def gate_kernel(x, weights, out_source, score_source, count_source, value_source, *rest):
    gate_out, base_out, out_w, counts, values, w, vector, block_count, sems = rest
    rows = x.shape[0]
    width = w.shape[1]
    model = out_w.shape[1]
    copies = [
        pltpu.make_async_copy(count_source, block_count, sems.at[3]),
        pltpu.make_async_copy(score_source, vector, sems.at[2]),
        pltpu.make_async_copy(weights.at[1], w, sems.at[0]),
        pltpu.make_async_copy(out_source, out_w, sems.at[1]),
        pltpu.make_async_copy(value_source, values, sems.at[4]),
    ]
    for copy in copies:
        copy.start()
    copies[0].wait()
    for b in range(block_count.shape[0]):
        counts[b : b + 1, :] = jnp.full((1, LANES), block_count[b], jnp.int32)
    copies[1].wait()
    chunks = model // LANES
    pieces = filled(split3(vector[...]), base_out.shape[0] - chunks * rows)
    base_out[chunks * rows :, :] = pieces.astype(BF16)
    copies[2].wait()
    gate = silu(jnp.dot(x[...], w[...], preferred_element_type=F32))
    gate_out[...] = gate
    copies[3].wait()
    base = jnp.dot(gate.astype(BF16), out_w[...], preferred_element_type=F32)
    for c in range(chunks):
        base_out[c * rows : (c + 1) * rows, :] = base[:, c * LANES : (c + 1) * LANES].astype(BF16)
    copies[4].wait()


def product_kernel(order, notes, gate, out_weight, *rest):
    owners = len(order)
    slots = {s: ref for s, ref in zip(order, rest)}
    full, sent = rest[owners:]
    rows, width = gate.shape
    chunks = out_weight.shape[1] // LANES
    blocks = rows // MOST
    size = slots[0].shape[1]
    heads = width // size
    group = LANES // MOST
    lines = [[jnp.zeros((1, LANES), F32)] * 7 for _ in range(-(-blocks // group))]
    gated = []
    for b in range(blocks):
        place = notes[b : b + 1, :size]
        picked = slots[0][...].astype(F32)
        for s in range(1, owners):
            picked = jnp.where(place == s, slots[s][...].astype(F32), picked)
        parts = [picked[h * MOST : (h + 1) * MOST] for h in range(heads)]
        extra = jnp.sum(sum(parts), axis=1, keepdims=True)
        centre = to_column(picked[heads * MOST : heads * MOST + 1], at_lane(0))
        square = jnp.sum(sum(part * part for part in parts), axis=1, keepdims=True)
        mask = at_lane(b % group * MOST)
        values = (
            to_line(centre, mask),
            *split3(to_line(extra, mask)),
            *split3(to_line(square, mask)),
        )
        lines[b // group] = [one + two for one, two in zip(lines[b // group], values)]
        gated.append(
            jnp.concatenate(
                [
                    part * gate[b * MOST : (b + 1) * MOST, h * size : (h + 1) * size]
                    for h, part in enumerate(parts)
                ],
                axis=1,
            )
        )
    product = jnp.dot(
        jnp.concatenate(gated, axis=0).astype(BF16), out_weight[...], preferred_element_type=F32
    )
    tail = filled([line for part in lines for line in part], sent.shape[0] - chunks * rows)
    for ref, kind in ((full, F32), (sent, BF16)):
        for c in range(chunks):
            ref[c * rows : (c + 1) * rows, :] = product[:, c * LANES : (c + 1) * LANES].astype(kind)
        ref[chunks * rows :, :] = tail.astype(kind)


def score_kernel(parts, counts, x, *rest):
    bases, products, out = rest[:parts], rest[parts : 2 * parts], rest[2 * parts]
    blocks, block_rows = out.shape
    rows, model = x.shape
    chunks = model // LANES
    own = chunks // parts
    group = LANES // MOST
    masks = [at_lane(b % group * MOST) for b in range(blocks)]
    tails = [p[chunks * rows :, :].astype(F32) for p in products]
    shifts, scales = [[] for _ in products], []
    for first in range(0, blocks, group):
        top = first // group * 7
        lines = [[tail[top + i : top + i + 1] for i in range(7)] for tail in tails]
        centres = [line[0] for line in lines]
        extras = [line[1] + line[2] + line[3] for line in lines]
        squares = [line[4] + line[5] + line[6] for line in lines]
        mean = sum(c * (model // parts) + e for c, e in zip(centres, extras)) / model
        deltas = [c - mean for c in centres]
        spread = sum(
            q + d * (2.0 * e + d * (model // parts)) for q, e, d in zip(squares, extras, deltas)
        )
        scale = lax.rsqrt(spread / model + EPSILON)
        for b in range(first, min(first + group, blocks)):
            scales.append(to_column(scale, masks[b]))
            for shift, delta in zip(shifts, deltas):
                shift.append(to_column(delta, masks[b]))
    offsets = [jnp.concatenate(shift, axis=0) for shift in shifts]
    scale = jnp.concatenate(scales, axis=0)
    me = lax.axis_index("mp")
    vectors = [base[chunks * rows :, :].astype(F32) for base in bases]
    vectors = [v[:own] + v[own : 2 * own] + v[2 * own : 3 * own] for v in vectors]
    score = jnp.zeros((rows, LANES), F32)
    for c in range(chunks):
        cut = slice(c * rows, (c + 1) * rows)
        total = sum(p[cut, :].astype(F32) for p in products)
        for d, base in zip(offsets, bases):
            total = total + d * base[cut, :].astype(F32)
        vector = vectors[0][c % own : c % own + 1]
        for s in range(1, parts):
            vector = jnp.where((me ^ s) == c // own, vectors[s][c % own : c % own + 1], vector)
        feature = x[:, c * LANES : (c + 1) * LANES].astype(F32)
        score = score + silu(feature + total * scale) * vector
    score = jnp.sum(score, axis=1, keepdims=True)
    mask = at_lane(0)
    lane = lax.broadcasted_iota(jnp.int32, (1, LANES), 1)
    for b in range(blocks):
        line = to_line(score[b * MOST : (b + 1) * MOST], mask)
        line = jnp.where(lane < counts[b : b + 1, :], line, 0.0)
        out[b : b + 1, :LANES] = line
        if block_rows > LANES:
            out[b : b + 1, LANES:] = jnp.zeros((1, block_rows - LANES), F32)


def swap(arrays, axis):
    size = lax.axis_size(axis)
    return [arrays[0]] + [
        lax.ppermute(arrays[s], axis, [(k, k ^ s) for k in range(size)]) for s in range(1, size)
    ]


def local(
    candidates,
    block_user,
    block_count,
    own_map,
    history_key_cache,
    cache_values,
    w_query_unit,
    time_bias,
    output_weight,
    w_score,
):
    owners = lax.axis_size("users")
    parts = lax.axis_size("mp")
    blocks, block_rows, model = candidates.shape
    users_here, _, width = history_key_cache.shape
    rows = blocks * MOST
    shape = jax.ShapeDtypeStruct

    def call(kernel, out_shape, in_specs, out_specs, scratch=()):
        return pl.pallas_call(
            kernel,
            out_shape=out_shape,
            in_specs=in_specs,
            out_specs=out_specs,
            scratch_shapes=list(scratch),
            compiler_params=pltpu.CompilerParams(vmem_limit_bytes=8 * 1024 * 1024),
        )

    def fetched(array):
        return pltpu.with_memory_space_constraint(array, pltpu.HBM)

    block_user, own_map, block_count = fetched(block_user), fetched(own_map), fetched(block_count)
    candidates, w_query_unit = fetched(candidates), fetched(w_query_unit)
    output_weight, value_cache = fetched(output_weight), fetched(cache_values)
    score_row = fetched(w_score.reshape(width // LANES, LANES))
    heads = time_bias.shape[0]
    chunks = model // LANES
    sums = (chunks * rows + whole_tiles(7 * -(-rows // LANES)), LANES)
    slot = shape((heads * MOST + TAIL, width // heads), BF16)
    notes_shape = shape((blocks, LANES), jnp.int32)
    *slots, x, notes = call(
        functools.partial(query_kernel, owners, users_here, heads),
        [slot] * owners + [shape((rows, model), BF16), notes_shape],
        [HBM] * 4,
        [VMEM] * (owners + 2),
        [
            pltpu.VMEM((model, width), BF16),
            pltpu.SMEM(block_user.shape, jnp.int32),
            pltpu.SMEM(own_map.shape, jnp.int32),
            pltpu.SemaphoreType.DMA((blocks,)),
            pltpu.SemaphoreType.DMA((CHUNKS,)),
            pltpu.SemaphoreType.DMA((2,)),
        ],
    )(block_user, own_map, candidates, w_query_unit)
    slots = swap(slots, "users")
    gate, base, out_w, counts, values = call(
        gate_kernel,
        [
            shape((rows, width), F32),
            shape((chunks * rows + whole_tiles(3 * width // LANES), LANES), BF16),
            shape(output_weight.shape, BF16),
            notes_shape,
            shape(cache_values.shape, BF16),
        ],
        [VMEM, HBM, HBM, HBM, HBM, HBM],
        [VMEM] * 5,
        [
            pltpu.VMEM((model, width), BF16),
            pltpu.VMEM((width // LANES, LANES), F32),
            pltpu.SMEM(block_count.shape, jnp.int32),
            pltpu.SemaphoreType.DMA((5,)),
        ],
    )(x, w_query_unit, output_weight, score_row, block_count, value_cache)
    bases = swap([base] * parts, "mp")

    def attend(order):
        return call(
            functools.partial(attend_kernel, len(order)),
            [slot] * len(order),
            [VMEM] * (3 + len(order)),
            [VMEM] * len(order),
        )(time_bias, history_key_cache, values, *[slots[s] for s in order])

    far_first = list(range(owners - 1, 0, -1))
    half_first = sorted(far_first, key=lambda s: s != owners // 2)
    mixtures = dict(zip([0], attend([0])))
    mixtures.update(zip(half_first, attend(half_first)))
    mixtures = swap(mixtures, "users")
    order = [*sorted(far_first, key=lambda s: s == owners // 2), 0]
    product, sent = call(
        functools.partial(product_kernel, order),
        [shape(sums, F32), shape(sums, BF16)],
        [VMEM] * (3 + owners),
        [VMEM] * 2,
    )(notes, gate, out_w, *[mixtures[s] for s in order])
    products = [product] + swap([sent] * parts, "mp")[1:]
    return call(
        functools.partial(score_kernel, parts),
        shape((blocks, block_rows), F32),
        [VMEM] * (2 + 2 * parts),
        VMEM,
    )(counts, x, *bases, *products)


def solution(mesh):
    return jax.shard_map(
        local,
        mesh=mesh,
        in_specs=(
            P(("groups", "users", "helpers"), None, None),
            P(("groups", "users", "helpers")),
            P(("groups", "users", "helpers")),
            P("groups"),
            P(("groups", "users"), None, "mp"),
            P(("groups", "users"), None, "mp"),
            P(None, None, "mp"),
            P("mp", None),
            P("mp", None),
            P("mp"),
        ),
        out_specs=P(("groups", "users", "helpers"), None),
        check_vma=False,
    )
```

```python
import functools

import jax
import jax.numpy as jnp
from jax import lax
from jax.experimental import pallas as pl
from jax.experimental.pallas import tpu as pltpu
from jax.sharding import PartitionSpec as P

EPSILON = 1e-05
MOST = 32
LANES = 128
TAIL = 16
CHUNKS = 4
F32 = jnp.float32
BF16 = jnp.bfloat16
VMEM = pl.BlockSpec(memory_space=pltpu.VMEM)
HBM = pl.BlockSpec(memory_space=pltpu.HBM)


def silu(v):
    return v / (1.0 + jnp.exp(-v))


def split3(v):
    high = v.astype(BF16).astype(F32)
    rest = v - high
    middle = rest.astype(BF16).astype(F32)
    return high, middle, rest - middle


def at_lane(shift):
    row = lax.broadcasted_iota(jnp.int32, (MOST, LANES), 0)
    return row + shift == lax.broadcasted_iota(jnp.int32, (MOST, LANES), 1)


def to_line(column, mask):
    return jnp.sum(jnp.where(mask, column, 0.0), axis=0, keepdims=True)


def to_column(line, mask):
    return jnp.sum(jnp.where(mask, line, 0.0), axis=1, keepdims=True)


def filled(pieces, rows):
    spare = rows - sum(piece.shape[0] for piece in pieces)
    none = [jnp.zeros((spare, LANES), F32)] if spare > 0 else []
    return jnp.concatenate([*pieces, *none], axis=0)


def whole_tiles(rows):
    return -(-rows // TAIL) * TAIL


def query_kernel(owners, users_here, heads, user_source, map_source, candidates, weights, *rest):
    slots, (x, notes) = rest[:owners], rest[owners : owners + 2]
    w, block_user, own_map, x_sems, w_sems, sems = rest[owners + 2 :]
    blocks = candidates.shape[0]
    model, width = w.shape
    size = width // heads
    part = model // CHUNKS
    small = [
        pltpu.make_async_copy(user_source, block_user, sems.at[0]),
        pltpu.make_async_copy(map_source, own_map, sems.at[1]),
    ]
    x_copies = [
        pltpu.make_async_copy(
            candidates.at[b, pl.ds(0, MOST)], x.at[pl.ds(b * MOST, MOST)], x_sems.at[b]
        )
        for b in range(blocks)
    ]
    w_copies = [
        pltpu.make_async_copy(
            weights.at[0, pl.ds(i * part, part)], w.at[pl.ds(i * part, part)], w_sems.at[i]
        )
        for i in range(CHUNKS)
    ]
    for copy in small + x_copies + w_copies:
        copy.start()
    for copy in small:
        copy.wait()
    me = lax.axis_index("users")
    homes = []
    for b in range(blocks):
        storage = own_map[block_user[b]]
        homes.append(((storage // users_here) ^ me, storage % users_here))
        notes[b : b + 1, :] = jnp.full((1, LANES), homes[b][0], jnp.int32)
    for copy in x_copies:
        copy.wait()
    query = jnp.zeros((blocks * MOST, width), F32)
    for i, copy in enumerate(w_copies):
        copy.wait()
        cut = slice(i * part, (i + 1) * part)
        query += jnp.dot(x[:, cut], w[cut, :], preferred_element_type=F32)
    query = silu(query).astype(BF16)
    for s in range(owners):
        tag = jnp.zeros((TAIL, size), F32)
        for b, (slot, row) in enumerate(homes):
            tag = jnp.where(slot == s, row.astype(F32), tag)
        for h in range(heads):
            piece = jnp.zeros((MOST, size), BF16)
            for b, (slot, row) in enumerate(homes):
                mine = query[b * MOST : (b + 1) * MOST, h * size : (h + 1) * size]
                piece = jnp.where(slot == s, mine, piece)
            slots[s][h * MOST : (h + 1) * MOST, :] = piece
        slots[s][heads * MOST :, :] = tag.astype(BF16)


def attend_kernel(count, bias, keys, values, *rest):
    slots, outs = rest[:count], rest[count:]
    users_here, history, width = keys.shape
    heads = bias.shape[0]
    size = width // heads
    scale = size ** (-0.5)
    rows, weights = [], []
    for s in range(count):
        tag = jnp.max(slots[s][heads * MOST :, :].astype(F32))
        row = jnp.clip(tag.astype(jnp.int32), 0, users_here - 1)
        rows.append(row)
    none = jnp.zeros((MOST, size), BF16)
    for s in range(count):
        for h in range(0, heads, 2):
            one = slots[s][h * MOST : (h + 1) * MOST, :]
            two = slots[s][(h + 1) * MOST : (h + 2) * MOST, :]
            query = jnp.concatenate(
                [jnp.concatenate([one, none], axis=1), jnp.concatenate([none, two], axis=1)], axis=0
            )
            logits = lax.dot_general(
                query,
                keys[rows[s], :, h * size : (h + 2) * size],
                (((1,), (1,)), ((), ())),
                preferred_element_type=F32,
            )
            pair = jnp.concatenate(
                [jnp.broadcast_to(bias[h + i : h + i + 1, :], (MOST, history)) for i in range(2)]
            )
            weights.append(silu(logits * scale + pair).astype(BF16))
    mask = at_lane(0)
    for s in range(count):
        parts = []
        for h in range(0, heads, 2):
            mixed = jnp.dot(
                weights[(s * heads + h) // 2],
                values[rows[s], :, h * size : (h + 2) * size],
                preferred_element_type=F32,
            )
            parts += [mixed[:MOST, :size], mixed[MOST:, size:]]
        mean = jnp.sum(sum(parts), axis=1, keepdims=True) / width
        mean = mean.astype(BF16).astype(F32)
        for h, part in enumerate(parts):
            outs[s][h * MOST : (h + 1) * MOST, :] = (part - mean).astype(BF16)
        outs[s][heads * MOST :, :] = jnp.broadcast_to(to_line(mean, mask), (TAIL, size)).astype(BF16)


def gate_kernel(x, weights, out_source, score_source, count_source, value_source, *rest):
    gate_out, base_out, out_w, counts, values, w, vector, block_count, sems = rest
    rows = x.shape[0]
    width = w.shape[1]
    model = out_w.shape[1]
    copies = [
        pltpu.make_async_copy(count_source, block_count, sems.at[3]),
        pltpu.make_async_copy(score_source, vector, sems.at[2]),
        pltpu.make_async_copy(weights.at[1], w, sems.at[0]),
        pltpu.make_async_copy(out_source, out_w, sems.at[1]),
        pltpu.make_async_copy(value_source, values, sems.at[4]),
    ]
    for copy in copies:
        copy.start()
    copies[0].wait()
    for b in range(block_count.shape[0]):
        counts[b : b + 1, :] = jnp.full((1, LANES), block_count[b], jnp.int32)
    copies[1].wait()
    chunks = model // LANES
    pieces = filled(split3(vector[...]), base_out.shape[0] - chunks * rows)
    base_out[chunks * rows :, :] = pieces.astype(BF16)
    copies[2].wait()
    gate = silu(jnp.dot(x[...], w[...], preferred_element_type=F32))
    gate_out[...] = gate
    copies[3].wait()
    base = jnp.dot(gate.astype(BF16), out_w[...], preferred_element_type=F32)
    for c in range(chunks):
        base_out[c * rows : (c + 1) * rows, :] = base[:, c * LANES : (c + 1) * LANES].astype(BF16)
    copies[4].wait()


def product_kernel(order, notes, gate, out_weight, *rest):
    owners = len(order)
    slots = {s: ref for s, ref in zip(order, rest)}
    (sent,) = rest[owners:]
    rows, width = gate.shape
    chunks = out_weight.shape[1] // LANES
    blocks = rows // MOST
    size = slots[0].shape[1]
    heads = width // size
    group = LANES // MOST
    lines = [[jnp.zeros((1, LANES), F32)] * 7 for _ in range(-(-blocks // group))]
    gated = []
    for b in range(blocks):
        place = notes[b : b + 1, :size]
        picked = slots[0][...].astype(F32)
        for s in range(1, owners):
            picked = jnp.where(place == s, slots[s][...].astype(F32), picked)
        parts = [picked[h * MOST : (h + 1) * MOST] for h in range(heads)]
        extra = jnp.sum(sum(parts), axis=1, keepdims=True)
        centre = to_column(picked[heads * MOST : heads * MOST + 1], at_lane(0))
        square = jnp.sum(sum(part * part for part in parts), axis=1, keepdims=True)
        mask = at_lane(b % group * MOST)
        values = (
            to_line(centre, mask),
            *split3(to_line(extra, mask)),
            *split3(to_line(square, mask)),
        )
        lines[b // group] = [one + two for one, two in zip(lines[b // group], values)]
        gated.append(
            jnp.concatenate(
                [
                    part * gate[b * MOST : (b + 1) * MOST, h * size : (h + 1) * size]
                    for h, part in enumerate(parts)
                ],
                axis=1,
            )
        )
    product = jnp.dot(
        jnp.concatenate(gated, axis=0).astype(BF16), out_weight[...], preferred_element_type=F32
    )
    tail = filled([line for part in lines for line in part], sent.shape[0] - chunks * rows)
    kind = sent.dtype
    for c in range(chunks):
        sent[c * rows : (c + 1) * rows, :] = product[:, c * LANES : (c + 1) * LANES].astype(kind)
    sent[chunks * rows :, :] = tail.astype(kind)


def score_kernel(parts, counts, x, *rest):
    bases, products, out = rest[:parts], rest[parts : 2 * parts], rest[2 * parts]
    blocks, block_rows = out.shape
    rows, model = x.shape
    chunks = model // LANES
    own = chunks // parts
    group = LANES // MOST
    masks = [at_lane(b % group * MOST) for b in range(blocks)]
    tails = [p[chunks * rows :, :].astype(F32) for p in products]
    shifts, scales = [[] for _ in products], []
    for first in range(0, blocks, group):
        top = first // group * 7
        lines = [[tail[top + i : top + i + 1] for i in range(7)] for tail in tails]
        centres = [line[0] for line in lines]
        extras = [line[1] + line[2] + line[3] for line in lines]
        squares = [line[4] + line[5] + line[6] for line in lines]
        mean = sum(c * (model // parts) + e for c, e in zip(centres, extras)) / model
        deltas = [c - mean for c in centres]
        spread = sum(
            q + d * (2.0 * e + d * (model // parts)) for q, e, d in zip(squares, extras, deltas)
        )
        scale = lax.rsqrt(spread / model + EPSILON)
        for b in range(first, min(first + group, blocks)):
            scales.append(to_column(scale, masks[b]))
            for shift, delta in zip(shifts, deltas):
                shift.append(to_column(delta, masks[b]))
    offsets = [jnp.concatenate(shift, axis=0) for shift in shifts]
    scale = jnp.concatenate(scales, axis=0)
    me = lax.axis_index("mp")
    vectors = [base[chunks * rows :, :].astype(F32) for base in bases]
    vectors = [v[:own] + v[own : 2 * own] + v[2 * own : 3 * own] for v in vectors]
    score = jnp.zeros((rows, LANES), F32)
    for c in range(chunks):
        cut = slice(c * rows, (c + 1) * rows)
        total = sum(p[cut, :].astype(F32) for p in products)
        for d, base in zip(offsets, bases):
            total = total + d * base[cut, :].astype(F32)
        vector = vectors[0][c % own : c % own + 1]
        for s in range(1, parts):
            vector = jnp.where((me ^ s) == c // own, vectors[s][c % own : c % own + 1], vector)
        feature = x[:, c * LANES : (c + 1) * LANES].astype(F32)
        score = score + silu(feature + total * scale) * vector
    score = jnp.sum(score, axis=1, keepdims=True)
    mask = at_lane(0)
    lane = lax.broadcasted_iota(jnp.int32, (1, LANES), 1)
    for b in range(blocks):
        line = to_line(score[b * MOST : (b + 1) * MOST], mask)
        line = jnp.where(lane < counts[b : b + 1, :], line, 0.0)
        out[b : b + 1, :LANES] = line
        if block_rows > LANES:
            out[b : b + 1, LANES:] = jnp.zeros((1, block_rows - LANES), F32)


def swap(arrays, axis):
    size = lax.axis_size(axis)
    return [arrays[0]] + [
        lax.ppermute(arrays[s], axis, [(k, k ^ s) for k in range(size)]) for s in range(1, size)
    ]


def local(
    candidates,
    block_user,
    block_count,
    own_map,
    history_key_cache,
    cache_values,
    w_query_unit,
    time_bias,
    output_weight,
    w_score,
):
    owners = lax.axis_size("users")
    parts = lax.axis_size("mp")
    blocks, block_rows, model = candidates.shape
    users_here, _, width = history_key_cache.shape
    rows = blocks * MOST
    shape = jax.ShapeDtypeStruct

    def call(kernel, out_shape, in_specs, out_specs, scratch=()):
        return pl.pallas_call(
            kernel,
            out_shape=out_shape,
            in_specs=in_specs,
            out_specs=out_specs,
            scratch_shapes=list(scratch),
            compiler_params=pltpu.CompilerParams(vmem_limit_bytes=8 * 1024 * 1024),
        )

    def fetched(array):
        return pltpu.with_memory_space_constraint(array, pltpu.HBM)

    block_user, own_map, block_count = fetched(block_user), fetched(own_map), fetched(block_count)
    candidates, w_query_unit = fetched(candidates), fetched(w_query_unit)
    output_weight, value_cache = fetched(output_weight), fetched(cache_values)
    score_row = fetched(w_score.reshape(width // LANES, LANES))
    heads = time_bias.shape[0]
    chunks = model // LANES
    sums = (chunks * rows + whole_tiles(7 * -(-rows // LANES)), LANES)
    slot = shape((heads * MOST + TAIL, width // heads), BF16)
    notes_shape = shape((blocks, LANES), jnp.int32)
    *slots, x, notes = call(
        functools.partial(query_kernel, owners, users_here, heads),
        [slot] * owners + [shape((rows, model), BF16), notes_shape],
        [HBM] * 4,
        [VMEM] * (owners + 2),
        [
            pltpu.VMEM((model, width), BF16),
            pltpu.SMEM(block_user.shape, jnp.int32),
            pltpu.SMEM(own_map.shape, jnp.int32),
            pltpu.SemaphoreType.DMA((blocks,)),
            pltpu.SemaphoreType.DMA((CHUNKS,)),
            pltpu.SemaphoreType.DMA((2,)),
        ],
    )(block_user, own_map, candidates, w_query_unit)
    slots = swap(slots, "users")
    gate, base, out_w, counts, values = call(
        gate_kernel,
        [
            shape((rows, width), F32),
            shape((chunks * rows + whole_tiles(3 * width // LANES), LANES), BF16),
            shape(output_weight.shape, BF16),
            notes_shape,
            shape(cache_values.shape, BF16),
        ],
        [VMEM, HBM, HBM, HBM, HBM, HBM],
        [VMEM] * 5,
        [
            pltpu.VMEM((model, width), BF16),
            pltpu.VMEM((width // LANES, LANES), F32),
            pltpu.SMEM(block_count.shape, jnp.int32),
            pltpu.SemaphoreType.DMA((5,)),
        ],
    )(x, w_query_unit, output_weight, score_row, block_count, value_cache)
    bases = swap([base] * parts, "mp")

    def attend(order):
        return call(
            functools.partial(attend_kernel, len(order)),
            [slot] * len(order),
            [VMEM] * (3 + len(order)),
            [VMEM] * len(order),
        )(time_bias, history_key_cache, values, *[slots[s] for s in order])

    far_first = list(range(owners - 1, 0, -1))
    half_first = sorted(far_first, key=lambda s: s != owners // 2)
    mixtures = dict(zip([0], attend([0])))
    mixtures.update(zip(half_first, attend(half_first)))
    mixtures = swap(mixtures, "users")
    order = [*far_first, 0]
    sent, product = (
        call(
            functools.partial(product_kernel, order),
            [shape(sums, kind)],
            [VMEM] * (3 + owners),
            [VMEM],
        )(notes, gate, out_w, *[mixtures[s] for s in order])[0]
        for kind in (BF16, F32)
    )
    products = [product] + swap([sent] * parts, "mp")[1:]
    return call(
        functools.partial(score_kernel, parts),
        shape((blocks, block_rows), F32),
        [VMEM] * (2 + 2 * parts),
        VMEM,
    )(counts, x, *bases, *products)


def solution(mesh):
    return jax.shard_map(
        local,
        mesh=mesh,
        in_specs=(
            P(("groups", "users", "helpers"), None, None),
            P(("groups", "users", "helpers")),
            P(("groups", "users", "helpers")),
            P("groups"),
            P(("groups", "users"), None, "mp"),
            P(("groups", "users"), None, "mp"),
            P(None, None, "mp"),
            P("mp", None),
            P("mp", None),
            P("mp"),
        ),
        out_specs=P(("groups", "users", "helpers"), None),
        check_vma=False,
    )
```
